32 devices in a mesh: groups: 2 (over x), tm: 16 (over z, y, core).
Axes of the slice: x: 2, y: 2, z: 4, core: 2. Of those that a mesh axis runs over, the one named last changes fastest.
Arguments:
- state: float32 [32, 64, 1, 1440], P(('groups', 'tm')), parts along dimension 0, may hold values from -18 to 18
- observed: float32 [32, 64, 1, 1440], P(('groups', 'tm')), parts along dimension 0, may hold values from -6 to 6
- obs_mask: int32 [32, 64, 1, 1440], P(('groups', 'tm')), parts along dimension 0, may hold values 0 or 1
- noise: float32 [32, 64, 1, 1440], P(('groups', 'tm')), parts along dimension 0, may hold values from -6 to 6
- w_first: bfloat16 [256, 320, 3, 3], replicated, may hold values from -0.109375 to 0.109375
- b_first: float32 [256], replicated, may hold values from -3 to 3
- w_second: bfloat16 [64, 256, 3, 3], replicated, may hold values from -0.125 to 0.125
- b_second: float32 [64], replicated, may hold values from -3 to 3
Outputs:
- sample: float32 [32, 64, 1, 1440], P(('groups', 'tm')), parts along dimension 0
The draws below stay inside these ranges and needn't reach their ends.
There are 2 independent parts, one for each index of `groups`. The reference program is written for one: setup_inputs(seed, part) draws one part's arguments, and reference() takes and returns one part's arrays. A program takes and returns all parts, laid end to end along the dimension named above; an argument that names none is the same for every part. Nothing has to cross between parts.
All inputs are finite; a program needn't handle non-finite values. No bound on the sum of `obs_mask` on one device may be relied on, other than what follows from the above.
Results may differ from the reference program's by a relative error of at most 0.00048.
Values may be sent and summed in bfloat16 or wider, within the bound.
A program may use at most 64 MiB of HBM per device.

```python
import jax
import jax.numpy as jnp
from jax import lax

VARS = 64
HID = 256
WIN = 5
LAT = 1
LON = 1440
HOURS = 16


def draw_state(key, part):
    key_a = jax.random.fold_in(key, 11)
    key_b = jax.random.fold_in(key, 12)
    hour_scale = 1.0 + 2.0 * jnp.arange(HOURS, dtype=jnp.float32) / max(HOURS - 1, 1)
    var_scale = jnp.exp(jax.random.uniform(key_b, (1, VARS, LAT, 1), jnp.float32, -0.69, 0.69))
    shape = (HOURS, VARS, LAT, LON)
    base = jnp.clip(jax.random.normal(key_a, shape, jnp.float32), -3.0, 3.0)
    return hour_scale[:, None, None, None] * var_scale * base


def set_ends(drawn, rng, least, high):
    extent = drawn.shape
    place = [jax.random.randint(jax.random.fold_in(rng, axis), (), 0, extent[axis]) for axis in range(len(extent))]
    drawn = drawn.at[tuple(place)].set(least)
    longest = extent.index(max(extent))
    place[longest] = (place[longest] + 1) % extent[longest]
    return drawn.at[tuple(place)].set(high)


def block_scale(own_key, extent, pieces, least, largest):
    def one(dim, blocks):
        draws = jax.random.uniform(jax.random.fold_in(jax.random.fold_in(own_key, 6), dim), (blocks,), jnp.float32, least / len(pieces), largest / len(pieces))
        return jnp.repeat(jnp.exp(draws), extent[dim] // blocks).reshape((-1,) + (1,) * (len(extent) - dim - 1))

    factor_of = one(*pieces[0])
    for cut in pieces[1:]:
        factor_of = factor_of * one(*cut)
    return factor_of


def centred(own_key, dims, scale, reach, split=(), kind=jnp.bfloat16):
    gain = block_scale(own_key, dims, split, -0.22, 0.18) if split else 1.0
    array = jax.random.normal(own_key, dims, jnp.float32) * scale * gain
    return jnp.minimum(jnp.maximum(array, -reach), reach).astype(kind)


def setup_inputs(seed: int = 0, part: int = 0) -> dict:
    key_list = jax.random.split(jax.random.key(seed), 9)
    part_splits = jax.random.split(jax.random.fold_in(key_list[8], part), 9)
    state = draw_state(jax.random.fold_in(jax.random.fold_in(key_list[8], part), 71), part)
    observed = centred(part_splits[1], (HOURS, VARS, LAT, LON), 1.0, 6.0, ((0, 16),), jnp.float32)
    obs_mask = set_ends((jax.random.randint(part_splits[2], (HOURS, VARS, LAT, LON), 0, 4) < 1).astype(jnp.int32), jax.random.fold_in(part_splits[2], 1), 0, 1)
    noise = centred(part_splits[3], (HOURS, VARS, LAT, LON), 1.0, 6.0, ((0, 16),), jnp.float32)
    w_first = centred(key_list[4], (HID, WIN * VARS, 3, 3), (9 * WIN * VARS) ** -0.5, 0.109375)
    b_first = centred(key_list[5], (HID,), 0.5, 3.0, (), jnp.float32)
    w_second = centred(key_list[6], (VARS, HID, 3, 3), (9 * HID) ** -0.5, 0.125)
    b_second = centred(key_list[7], (VARS,), 0.5, 3.0, (), jnp.float32)
    return {"state": state, "observed": observed, "obs_mask": obs_mask, "noise": noise, "w_first": w_first, "b_first": b_first, "w_second": w_second, "b_second": b_second}


def conv_wrap(field, weights):
    wrapped = jnp.concatenate([field[..., -1:], field, field[..., :1]], axis=-1)
    padded = jnp.pad(wrapped, ((0, 0), (0, 0), (1, 1), (0, 0)))
    return lax.conv_general_dilated(padded, weights, (1, 1), 'VALID', dimension_numbers=('NCHW', 'OIHW', 'NCHW'), preferred_element_type=jnp.float32)

def score(field, observed, mask_f, w_first, b_first, w_second, b_second):
    rounded = field.astype(jnp.bfloat16)
    padded = jnp.pad(rounded, ((2, 2), (0, 0), (0, 0), (0, 0)))
    window = jnp.concatenate([padded[k:k + HOURS] for k in range(WIN)], axis=1)
    pre = conv_wrap(window, w_first) + b_first[None, :, None, None]
    hidden = jax.nn.silu(pre).astype(jnp.bfloat16)
    out = conv_wrap(hidden, w_second) + b_second[None, :, None, None]
    return out + mask_f * (observed - field)

def reference(state, observed, obs_mask, noise, w_first, b_first, w_second, b_second):
    mask_f = obs_mask.astype(jnp.float32)
    predicted = state + 0.5 * score(state, observed, mask_f, w_first, b_first, w_second, b_second)
    drift = score(predicted, observed, mask_f, w_first, b_first, w_second, b_second)
    zsq = jnp.sum(noise * noise)
    gsq = jnp.sum(drift * drift)
    step = 2.0 * 0.16 * 0.16 * zsq / (gsq + 1e-06)
    return predicted + step * drift + jnp.sqrt(2.0 * step) * noise
```

```python
import functools

import jax
import jax.numpy as jnp
from jax import lax
from jax.experimental import pallas as pl
from jax.experimental.pallas import tpu as pltpu
from jax.sharding import PartitionSpec as P

CHUNKS = 3
LANES = 128


def cut(field, chunks, useful, halo):
    lon = field.shape[-1]
    pieces = []
    for c in range(chunks):
        lo, hi = c * useful - halo, (c + 1) * useful + halo
        parts = []
        if lo < 0:
            parts.append(field[:, lon + lo :])
        parts.append(field[:, max(lo, 0) : min(hi, lon)])
        if hi > lon:
            parts.append(field[:, : hi - lon])
        pieces.append(jnp.concatenate(parts, axis=1) if len(parts) > 1 else parts[0])
    return pieces


def kernel(
    n, chunks, useful, halo,
    state_hbm, obs_hbm, mask_hbm, noise_hbm, w1_hbm, b1_ref, w2_hbm, b2_ref, out_ref,
    state_v, obs_v, mask_v, noise_v, w1_v, w2_v,
    w1t, b1t, b2t, fld, inn, drift, win, sums,
    local_sem, send_sem, recv_sem, sum_send, sum_recv,
):
    me = lax.axis_index("tm")
    group = lax.axis_index("groups")
    core = lax.rem(me, 2)
    par = lax.rem(me // 2, 2)
    sib = me + 1 - 2 * core
    partner = me + 2 - 4 * par
    onward = me + 4 - 8 * par
    near, far = 4 - 4 * par, 4 * par
    relay = 4 - 4 * core
    has_far = jnp.logical_or(jnp.logical_and(par == 0, me >= 4), jnp.logical_and(par == 1, me + 4 < n))
    has_onward = jnp.logical_or(jnp.logical_and(par == 0, me + 4 < n), jnp.logical_and(par == 1, me >= 4))
    nvars = fld.shape[1]
    hid = w1t.shape[0]
    width = fld.shape[2]

    barrier = pltpu.get_barrier_semaphore()

    @pl.loop(1, n)
    def _(d):
        pl.semaphore_signal(
            barrier, inc=1, device_id=(group, lax.rem(me + d, n)), device_id_type=pl.DeviceIdType.MESH
        )

    loads = []
    for i, (src, dst) in enumerate(
        (
            (state_hbm, state_v),
            (w1_hbm.at[w1_hbm.shape[0] // 2], w1_v),
            (w2_hbm.at[w2_hbm.shape[0] // 2], w2_v),
            (obs_hbm, obs_v),
            (mask_hbm, mask_v),
            (noise_hbm, noise_v),
        )
    ):
        loads.append(pltpu.make_async_copy(src, dst, local_sem.at[i]))
        loads[-1].start()

    def remote(step, kind, src, dst, device):
        return pltpu.make_async_remote_copy(
            src_ref=win.at[step, src],
            dst_ref=win.at[step, dst],
            send_sem=send_sem.at[step, kind],
            recv_sem=recv_sem.at[step, kind],
            device_id=(group, device),
            device_id_type=pl.DeviceIdType.MESH,
        )

    def direct(step):
        return remote(step, 0, 2, far, partner)

    def forward(step):
        return remote(step, 1, near, far, onward)

    def own_to_sib(step):
        return remote(step, 2, 2, 1 + 2 * core, sib)

    def relay_to_sib(step):
        return remote(step, 3, relay, 3 - 2 * core, sib)

    @pl.when(jnp.logical_not(has_far))
    def _():
        for step in range(2 * chunks):
            win[step, far] = jnp.zeros((nvars, width), jnp.bfloat16)

    @pl.when(jnp.logical_and(jnp.logical_not(has_far), core == par))
    def _():
        for step in range(2 * chunks):
            win[step, 1 + 2 * core] = jnp.zeros((nvars, width), jnp.bfloat16)

    loads[0].wait()
    for c, piece in enumerate(cut(state_v[...], chunks, useful, halo)):
        fld[c] = piece
        win[c, 2] = piece.astype(jnp.bfloat16)

    pl.semaphore_wait(barrier, n - 1)
    for c in range(chunks):
        direct(c).start()
        own_to_sib(c).start()

    loads[1].wait()
    rows = []
    for slot in range(5):
        for tap in range(3):
            rows.append(w1_v[tap, slot * nvars : (slot + 1) * nvars, :])
    stacked = jnp.concatenate(rows, axis=0).astype(jnp.float32)
    w1t[...] = stacked.T.astype(jnp.bfloat16)
    b1t[...] = jnp.broadcast_to(b1_ref[...], (LANES, hid)).T
    b2t[...] = jnp.broadcast_to(b2_ref[...], (LANES, nvars)).T
    loads[2].wait()
    loads[3].wait()
    loads[4].wait()
    loads[5].wait()
    mask_pieces = cut(mask_v[...].astype(jnp.float32), chunks, useful, halo)
    obs_pieces = cut(obs_v[...], chunks, useful, halo)
    for c in range(chunks):
        inn[0, c] = mask_pieces[c]
        inn[1, c] = obs_pieces[c]
    noise = noise_v[...]
    zsq = jnp.sum(noise * noise)

    def arrive(step):
        direct(step).wait_recv()

        @pl.when(has_onward)
        def _():
            forward(step).start()

        @pl.when(core == par)
        def _():
            relay_to_sib(step).start()

    def arrive_far(step):
        @pl.when(has_far)
        def _():
            forward(step).wait_recv()

            @pl.when(core != par)
            def _():
                relay_to_sib(step).start()

    def work(step):
        own_to_sib(step).wait_recv()

        @pl.when(jnp.logical_or(core != par, has_far))
        def _():
            relay_to_sib(step).wait_recv()

        c = step % chunks
        rows = []
        for slot in range(5):
            x = win[step, slot]
            xf = x.astype(jnp.float32)
            rows.append(pltpu.roll(xf, 1, 1).astype(jnp.bfloat16))
            rows.append(x)
            rows.append(pltpu.roll(xf, width - 1, 1).astype(jnp.bfloat16))
        pre = jnp.dot(w1t[...], jnp.concatenate(rows, axis=0), preferred_element_type=jnp.float32)
        pre = pre + b1t[:, :1]
        hidden = (0.5 * pre * (1.0 + jnp.tanh(0.5 * pre))).astype(jnp.bfloat16)
        y = jnp.dot(
            w2_v[...].reshape(3 * nvars, hid), hidden, preferred_element_type=jnp.float32
        )
        out = pltpu.roll(y[:nvars], 1, 1) + y[nvars : 2 * nvars] + pltpu.roll(y[2 * nvars :], width - 1, 1)
        field = fld[c]
        return field, out + b2t[:, :1] + inn[0, c] * (inn[1, c] - field)

    gsq = jnp.zeros((nvars, width), jnp.float32)
    lane = lax.broadcasted_iota(jnp.int32, (nvars, width), 1)
    valid = jnp.logical_and(lane >= halo, lane < halo + useful)
    steps = 2 * chunks
    for k in range(-2, steps):
        if 0 <= k + 2 < steps:
            arrive(k + 2)
        if 0 <= k + 1 < steps:
            arrive_far(k + 1)
        if k < 0:
            continue
        field, score = work(k)
        if k < chunks:
            field = field + 0.5 * score
            fld[k] = field
            win[k + chunks, 2] = field.astype(jnp.bfloat16)
            direct(k + chunks).start()
            own_to_sib(k + chunks).start()
        else:
            drift[k - chunks] = score
            gsq = gsq + jnp.where(valid, score * score, 0.0)

    row = lax.broadcasted_iota(jnp.int32, (8, LANES), 0)
    sums[me] = jnp.where(row == 0, zsq, jnp.sum(gsq))

    def share(device, slot):
        return pltpu.make_async_remote_copy(
            src_ref=sums.at[me],
            dst_ref=sums.at[slot],
            send_sem=sum_send.at[device],
            recv_sem=sum_recv.at[slot],
            device_id=(group, device),
            device_id_type=pl.DeviceIdType.MESH,
        )

    @pl.loop(1, n)
    def _(d):
        share(lax.rem(me + d, n), me).start()

    @pl.loop(1, n)
    def _(d):
        other = lax.rem(me + d, n)
        share(other, other).wait_recv()

    tot = jnp.sum(sums[...], axis=0)
    zall = tot[0:1, 0:1]
    gall = tot[1:2, 0:1]
    size = 2.0 * 0.16 * 0.16 * zall / (gall + 1e-06)
    scale = jnp.sqrt(2.0 * size)
    for c in range(chunks):
        piece = fld[c] + size * drift[c]
        span = slice(c * useful, (c + 1) * useful)
        out_ref[:, span] = piece[:, halo : halo + useful] + scale * noise_v[:, span]

    @pl.loop(1, n)
    def _(d):
        share(lax.rem(me + d, n), me).wait_send()

    for step in range(steps):
        direct(step).wait_send()
        own_to_sib(step).wait_send()

        @pl.when(has_onward)
        def _():
            forward(step).wait_send()

        @pl.when(jnp.logical_or(core == par, has_far))
        def _():
            relay_to_sib(step).wait_send()


def on_device(n, state, observed, obs_mask, noise, w_first, b_first, w_second, b_second):
    hours, nvars, lat, lon = state.shape
    hid = w_first.shape[0]
    assert hours == 1 and lat == 1 and n % 4 == 0
    assert w_first.shape[1:] == (5 * nvars, 3, 3)
    chunks = CHUNKS
    padded = -(-(lon + 8 * chunks) // (LANES * chunks)) * LANES * chunks
    width = padded // chunks
    assert lon % chunks == 0
    useful = lon // chunks
    halo = (width - useful) // 2
    assert halo >= 4 and useful + 2 * halo == width and halo <= useful
    flat = lambda a: a.reshape(nvars, lon)
    any_spec = pl.BlockSpec(memory_space=pl.ANY)
    vmem = pl.BlockSpec(memory_space=pltpu.VMEM)
    steps = 2 * chunks
    flops = 4 * width * chunks * hid * nvars * (15 + 3)
    out = pl.pallas_call(
        functools.partial(kernel, n, chunks, useful, halo),
        out_shape=jax.ShapeDtypeStruct((nvars, lon), jnp.float32),
        in_specs=[any_spec] * 5 + [vmem, any_spec, vmem],
        out_specs=vmem,
        scratch_shapes=[
            pltpu.VMEM((nvars, lon), jnp.float32),
            pltpu.VMEM((nvars, lon), jnp.float32),
            pltpu.VMEM((nvars, lon), jnp.int32),
            pltpu.VMEM((nvars, lon), jnp.float32),
            pltpu.VMEM((3, 5 * nvars, hid), jnp.bfloat16),
            pltpu.VMEM((3, nvars, hid), jnp.bfloat16),
            pltpu.VMEM((hid, 15 * nvars), jnp.bfloat16),
            pltpu.VMEM((hid, LANES), jnp.float32),
            pltpu.VMEM((nvars, LANES), jnp.float32),
            pltpu.VMEM((chunks, nvars, width), jnp.float32),
            pltpu.VMEM((2, chunks, nvars, width), jnp.float32),
            pltpu.VMEM((chunks, nvars, width), jnp.float32),
            pltpu.VMEM((steps, 5, nvars, width), jnp.bfloat16),
            pltpu.VMEM((n, 8, LANES), jnp.float32),
            pltpu.SemaphoreType.DMA((6,)),
            pltpu.SemaphoreType.DMA((steps, 4)),
            pltpu.SemaphoreType.DMA((steps, 4)),
            pltpu.SemaphoreType.DMA((n,)),
            pltpu.SemaphoreType.DMA((n,)),
        ],
        compiler_params=pltpu.CompilerParams(
            collective_id=0, has_side_effects=True, vmem_limit_bytes=40 * 1024 * 1024
        ),
        cost_estimate=pl.CostEstimate(flops=flops, bytes_accessed=4 * 1024 * 1024, transcendentals=0),
    )(
        flat(state),
        flat(observed),
        flat(obs_mask),
        flat(noise),
        jnp.transpose(w_first, (2, 3, 1, 0)),
        b_first.reshape(1, hid),
        jnp.transpose(w_second, (2, 3, 0, 1)),
        b_second.reshape(1, nvars),
    )
    return out.reshape(state.shape)


def solution(mesh):
    part = P(("groups", "tm"), None, None, None)
    return jax.shard_map(
        functools.partial(on_device, mesh.shape["tm"]),
        mesh=mesh,
        in_specs=(part, part, part, part, P(), P(), P(), P()),
        out_specs=part,
        check_vma=False,
    )
```

```python
import functools

import jax
import jax.numpy as jnp
from jax import lax
from jax.experimental import pallas as pl
from jax.experimental.pallas import tpu as pltpu
from jax.sharding import PartitionSpec as P

CHUNKS = 6
LANES = 128


def cut(field, chunks, useful, halo):
    lon = field.shape[-1]
    pieces = []
    for c in range(chunks):
        lo, hi = c * useful - halo, (c + 1) * useful + halo
        parts = []
        if lo < 0:
            parts.append(field[:, lon + lo :])
        parts.append(field[:, max(lo, 0) : min(hi, lon)])
        if hi > lon:
            parts.append(field[:, : hi - lon])
        pieces.append(jnp.concatenate(parts, axis=1) if len(parts) > 1 else parts[0])
    return pieces


def kernel(
    n, chunks, useful, halo,
    state_hbm, obs_hbm, mask_hbm, noise_hbm, w1_hbm, b1_ref, w2_hbm, b2_ref, out_ref,
    state_v, obs_v, mask_v, noise_v, w1_v, w2_v,
    w1t, b1t, b2t, fld, inn, drift, win, sums,
    local_sem, send_sem, recv_sem, sum_send, sum_recv,
):
    me = lax.axis_index("tm")
    group = lax.axis_index("groups")
    core = lax.rem(me, 2)
    par = lax.rem(me // 2, 2)
    sib = me + 1 - 2 * core
    partner = me + 2 - 4 * par
    onward = me + 4 - 8 * par
    near, far = 4 - 4 * par, 4 * par
    relay = 4 - 4 * core
    has_far = jnp.logical_or(jnp.logical_and(par == 0, me >= 4), jnp.logical_and(par == 1, me + 4 < n))
    has_onward = jnp.logical_or(jnp.logical_and(par == 0, me + 4 < n), jnp.logical_and(par == 1, me >= 4))
    nvars = fld.shape[1]
    hid = w1t.shape[0]
    width = fld.shape[2]

    barrier = pltpu.get_barrier_semaphore()

    @pl.loop(1, n)
    def _(d):
        pl.semaphore_signal(
            barrier, inc=1, device_id=(group, lax.rem(me + d, n)), device_id_type=pl.DeviceIdType.MESH
        )

    loads = []
    for i, (src, dst) in enumerate(
        (
            (state_hbm, state_v),
            (w1_hbm.at[w1_hbm.shape[0] // 2], w1_v),
            (w2_hbm.at[w2_hbm.shape[0] // 2], w2_v),
            (obs_hbm, obs_v),
            (mask_hbm, mask_v),
            (noise_hbm, noise_v),
        )
    ):
        loads.append(pltpu.make_async_copy(src, dst, local_sem.at[i]))
        loads[-1].start()

    def remote(step, kind, src, dst, device):
        return pltpu.make_async_remote_copy(
            src_ref=win.at[step, src],
            dst_ref=win.at[step, dst],
            send_sem=send_sem.at[step, kind],
            recv_sem=recv_sem.at[step, kind],
            device_id=(group, device),
            device_id_type=pl.DeviceIdType.MESH,
        )

    def direct(step):
        return remote(step, 0, 2, far, partner)

    def forward(step):
        return remote(step, 1, near, far, onward)

    def own_to_sib(step):
        return remote(step, 2, 2, 1 + 2 * core, sib)

    def relay_to_sib(step):
        return remote(step, 3, relay, 3 - 2 * core, sib)

    @pl.when(jnp.logical_not(has_far))
    def _():
        for step in range(2 * chunks):
            win[step, far] = jnp.zeros((nvars, width), jnp.bfloat16)

    @pl.when(jnp.logical_and(jnp.logical_not(has_far), core == par))
    def _():
        for step in range(2 * chunks):
            win[step, 1 + 2 * core] = jnp.zeros((nvars, width), jnp.bfloat16)

    loads[0].wait()
    for c, piece in enumerate(cut(state_v[...], chunks, useful, halo)):
        fld[c] = piece
        win[c, 2] = piece.astype(jnp.bfloat16)

    pl.semaphore_wait(barrier, n - 1)
    for c in range(chunks):
        direct(c).start()
        own_to_sib(c).start()

    loads[1].wait()
    rows = []
    for slot in range(5):
        for tap in range(3):
            rows.append(w1_v[tap, slot * nvars : (slot + 1) * nvars, :])
    stacked = jnp.concatenate(rows, axis=0).astype(jnp.float32)
    w1t[...] = stacked.T.astype(jnp.bfloat16)
    b1t[...] = jnp.broadcast_to(b1_ref[...], (LANES, hid)).T
    b2t[...] = jnp.broadcast_to(b2_ref[...], (LANES, nvars)).T
    loads[2].wait()
    loads[3].wait()
    loads[4].wait()
    loads[5].wait()
    mask_pieces = cut(mask_v[...].astype(jnp.float32), chunks, useful, halo)
    obs_pieces = cut(obs_v[...], chunks, useful, halo)
    for c in range(chunks):
        inn[0, c] = mask_pieces[c]
        inn[1, c] = obs_pieces[c]
    noise = noise_v[...]
    zsq = jnp.sum(noise * noise)

    def arrive(step):
        direct(step).wait_recv()

        @pl.when(has_onward)
        def _():
            forward(step).start()

        @pl.when(core == par)
        def _():
            relay_to_sib(step).start()

    def arrive_far(step):
        @pl.when(has_far)
        def _():
            forward(step).wait_recv()

            @pl.when(core != par)
            def _():
                relay_to_sib(step).start()

    def work(step):
        own_to_sib(step).wait_recv()

        @pl.when(jnp.logical_or(core != par, has_far))
        def _():
            relay_to_sib(step).wait_recv()

        c = step % chunks
        rows = []
        for slot in range(5):
            x = win[step, slot]
            xf = x.astype(jnp.float32)
            rows.append(pltpu.roll(xf, 1, 1).astype(jnp.bfloat16))
            rows.append(x)
            rows.append(pltpu.roll(xf, width - 1, 1).astype(jnp.bfloat16))
        pre = jnp.dot(w1t[...], jnp.concatenate(rows, axis=0), preferred_element_type=jnp.float32)
        pre = pre + b1t[:, :1]
        hidden = (0.5 * pre * (1.0 + jnp.tanh(0.5 * pre))).astype(jnp.bfloat16)
        y = jnp.dot(
            w2_v[...].reshape(3 * nvars, hid), hidden, preferred_element_type=jnp.float32
        )
        out = pltpu.roll(y[:nvars], 1, 1) + y[nvars : 2 * nvars] + pltpu.roll(y[2 * nvars :], width - 1, 1)
        field = fld[c]
        return field, out + b2t[:, :1] + inn[0, c] * (inn[1, c] - field)

    gsq = jnp.zeros((nvars, width), jnp.float32)
    lane = lax.broadcasted_iota(jnp.int32, (nvars, width), 1)
    valid = jnp.logical_and(lane >= halo, lane < halo + useful)
    steps = 2 * chunks
    for k in range(-2, steps):
        if 0 <= k + 2 < steps:
            arrive(k + 2)
        if 0 <= k + 1 < steps:
            arrive_far(k + 1)
        if k < 0:
            continue
        field, score = work(k)
        if k < chunks:
            field = field + 0.5 * score
            fld[k] = field
            win[k + chunks, 2] = field.astype(jnp.bfloat16)
            direct(k + chunks).start()
            own_to_sib(k + chunks).start()
        else:
            drift[k - chunks] = score
            gsq = gsq + jnp.where(valid, score * score, 0.0)

    row = lax.broadcasted_iota(jnp.int32, (8, LANES), 0)
    sums[me] = jnp.where(row == 0, zsq, jnp.sum(gsq))

    def share(device, slot):
        return pltpu.make_async_remote_copy(
            src_ref=sums.at[me],
            dst_ref=sums.at[slot],
            send_sem=sum_send.at[device],
            recv_sem=sum_recv.at[slot],
            device_id=(group, device),
            device_id_type=pl.DeviceIdType.MESH,
        )

    @pl.loop(1, n)
    def _(d):
        share(lax.rem(me + d, n), me).start()

    @pl.loop(1, n)
    def _(d):
        other = lax.rem(me + d, n)
        share(other, other).wait_recv()

    tot = jnp.sum(sums[...], axis=0)
    zall = tot[0:1, 0:1]
    gall = tot[1:2, 0:1]
    size = 2.0 * 0.16 * 0.16 * zall / (gall + 1e-06)
    scale = jnp.sqrt(2.0 * size)
    for c in range(chunks):
        piece = fld[c] + size * drift[c]
        span = slice(c * useful, (c + 1) * useful)
        out_ref[:, span] = piece[:, halo : halo + useful] + scale * noise_v[:, span]

    @pl.loop(1, n)
    def _(d):
        share(lax.rem(me + d, n), me).wait_send()

    for step in range(steps):
        direct(step).wait_send()
        own_to_sib(step).wait_send()

        @pl.when(has_onward)
        def _():
            forward(step).wait_send()

        @pl.when(jnp.logical_or(core == par, has_far))
        def _():
            relay_to_sib(step).wait_send()


def on_device(n, state, observed, obs_mask, noise, w_first, b_first, w_second, b_second):
    hours, nvars, lat, lon = state.shape
    hid = w_first.shape[0]
    assert hours == 1 and lat == 1 and n % 4 == 0
    assert w_first.shape[1:] == (5 * nvars, 3, 3)
    chunks = CHUNKS
    padded = -(-(lon + 8 * chunks) // (LANES * chunks)) * LANES * chunks
    width = padded // chunks
    assert lon % chunks == 0
    useful = lon // chunks
    halo = (width - useful) // 2
    assert halo >= 4 and useful + 2 * halo == width and halo <= useful
    flat = lambda a: a.reshape(nvars, lon)
    any_spec = pl.BlockSpec(memory_space=pl.ANY)
    vmem = pl.BlockSpec(memory_space=pltpu.VMEM)
    steps = 2 * chunks
    flops = 4 * width * chunks * hid * nvars * (15 + 3)
    out = pl.pallas_call(
        functools.partial(kernel, n, chunks, useful, halo),
        out_shape=jax.ShapeDtypeStruct((nvars, lon), jnp.float32),
        in_specs=[any_spec] * 5 + [vmem, any_spec, vmem],
        out_specs=vmem,
        scratch_shapes=[
            pltpu.VMEM((nvars, lon), jnp.float32),
            pltpu.VMEM((nvars, lon), jnp.float32),
            pltpu.VMEM((nvars, lon), jnp.int32),
            pltpu.VMEM((nvars, lon), jnp.float32),
            pltpu.VMEM((3, 5 * nvars, hid), jnp.bfloat16),
            pltpu.VMEM((3, nvars, hid), jnp.bfloat16),
            pltpu.VMEM((hid, 15 * nvars), jnp.bfloat16),
            pltpu.VMEM((hid, LANES), jnp.float32),
            pltpu.VMEM((nvars, LANES), jnp.float32),
            pltpu.VMEM((chunks, nvars, width), jnp.float32),
            pltpu.VMEM((2, chunks, nvars, width), jnp.float32),
            pltpu.VMEM((chunks, nvars, width), jnp.float32),
            pltpu.VMEM((steps, 5, nvars, width), jnp.bfloat16),
            pltpu.VMEM((n, 8, LANES), jnp.float32),
            pltpu.SemaphoreType.DMA((6,)),
            pltpu.SemaphoreType.DMA((steps, 4)),
            pltpu.SemaphoreType.DMA((steps, 4)),
            pltpu.SemaphoreType.DMA((n,)),
            pltpu.SemaphoreType.DMA((n,)),
        ],
        compiler_params=pltpu.CompilerParams(
            collective_id=0, has_side_effects=True, vmem_limit_bytes=40 * 1024 * 1024
        ),
        cost_estimate=pl.CostEstimate(flops=flops, bytes_accessed=4 * 1024 * 1024, transcendentals=0),
    )(
        flat(state),
        flat(observed),
        flat(obs_mask),
        flat(noise),
        jnp.transpose(w_first, (2, 3, 1, 0)),
        b_first.reshape(1, hid),
        jnp.transpose(w_second, (2, 3, 0, 1)),
        b_second.reshape(1, nvars),
    )
    return out.reshape(state.shape)


def solution(mesh):
    part = P(("groups", "tm"), None, None, None)
    return jax.shard_map(
        functools.partial(on_device, mesh.shape["tm"]),
        mesh=mesh,
        in_specs=(part, part, part, part, P(), P(), P(), P()),
        out_specs=part,
        check_vma=False,
    )
```

```python
import functools

import jax
import jax.numpy as jnp
from jax import lax
from jax.experimental import pallas as pl
from jax.experimental.pallas import tpu as pltpu
from jax.sharding import PartitionSpec as P

CHUNKS = 6
LANES = 128
ROWS = 16


def cut(field, chunks, useful, halo):
    lon = field.shape[-1]
    pieces = []
    for c in range(chunks):
        lo, hi = c * useful - halo, (c + 1) * useful + halo
        parts = []
        if lo < 0:
            parts.append(field[:, lon + lo :])
        parts.append(field[:, max(lo, 0) : min(hi, lon)])
        if hi > lon:
            parts.append(field[:, : hi - lon])
        pieces.append(jnp.concatenate(parts, axis=1) if len(parts) > 1 else parts[0])
    return pieces


def kernel(
    n, chunks, useful, halo,
    state_hbm, obs_hbm, mask_hbm, noise_hbm, w1_hbm, b1_ref, w2_hbm, b2_ref, out_ref,
    state_v, obs_v, mask_v, noise_v, w1_v, w2_v,
    w1t, b1t, b2t, fld, inn, drift, gacc, win, sums,
    local_sem, send_sem, recv_sem, sum_send, sum_recv,
):
    me = lax.axis_index("tm")
    group = lax.axis_index("groups")
    core = lax.rem(me, 2)
    par = lax.rem(me // 2, 2)
    sib = me + 1 - 2 * core
    partner = me + 2 - 4 * par
    onward = me + 4 - 8 * par
    near, far = 4 - 4 * par, 4 * par
    relay = 4 - 4 * core
    has_far = jnp.logical_or(jnp.logical_and(par == 0, me >= 4), jnp.logical_and(par == 1, me + 4 < n))
    has_onward = jnp.logical_or(jnp.logical_and(par == 0, me + 4 < n), jnp.logical_and(par == 1, me >= 4))
    nvars = fld.shape[1]
    hid = w1t.shape[1]
    width = fld.shape[2]
    steps = 2 * chunks

    barrier = pltpu.get_barrier_semaphore()

    @pl.loop(1, n)
    def _(d):
        pl.semaphore_signal(
            barrier, inc=1, device_id=(group, lax.rem(me + d, n)), device_id_type=pl.DeviceIdType.MESH
        )

    loads = []
    for i, (src, dst) in enumerate(
        (
            (state_hbm, state_v),
            (w1_hbm.at[w1_hbm.shape[0] // 2], w1_v),
            (w2_hbm.at[w2_hbm.shape[0] // 2], w2_v),
            (obs_hbm, obs_v),
            (mask_hbm, mask_v),
            (noise_hbm, noise_v),
        )
    ):
        loads.append(pltpu.make_async_copy(src, dst, local_sem.at[i]))
        loads[-1].start()

    def remote(step, kind, src, dst, device):
        return pltpu.make_async_remote_copy(
            src_ref=win.at[step, src],
            dst_ref=win.at[step, dst],
            send_sem=send_sem.at[step, kind],
            recv_sem=recv_sem.at[step, kind],
            device_id=(group, device),
            device_id_type=pl.DeviceIdType.MESH,
        )

    def direct(step):
        return remote(step, 0, 2, far, partner)

    def forward(step):
        return remote(step, 1, near, far, onward)

    def own_to_sib(step):
        return remote(step, 2, 2, 1 + 2 * core, sib)

    def relay_to_sib(step):
        return remote(step, 3, relay, 3 - 2 * core, sib)

    @pl.when(jnp.logical_not(has_far))
    def _():
        @pl.loop(0, steps)
        def _(step):
            win[step, far] = jnp.zeros((nvars, width), jnp.bfloat16)

    @pl.when(jnp.logical_and(jnp.logical_not(has_far), core == par))
    def _():
        @pl.loop(0, steps)
        def _(step):
            win[step, 1 + 2 * core] = jnp.zeros((nvars, width), jnp.bfloat16)

    loads[0].wait()

    @pl.loop(0, nvars // ROWS)
    def _(i):
        rows = pl.ds(pl.multiple_of(i * ROWS, ROWS), ROWS)
        for c, piece in enumerate(cut(state_v[rows, 0, :], chunks, useful, halo)):
            fld[c, rows] = piece
            win[c, 2, rows] = piece.astype(jnp.bfloat16)

    pl.semaphore_wait(barrier, n - 1)

    @pl.loop(0, chunks)
    def _(c):
        direct(c).start()
        own_to_sib(c).start()

    loads[1].wait()

    @pl.loop(0, 5)
    def _(slot):
        rows = pl.ds(pl.multiple_of(slot * nvars, nvars), nvars)
        stacked = jnp.concatenate([w1_v[tap, rows, :] for tap in range(3)], axis=0)
        w1t[slot] = stacked.astype(jnp.float32).T.astype(jnp.bfloat16)

    b1t[...] = jnp.broadcast_to(b1_ref[...], (LANES, hid)).T
    b2t[...] = jnp.broadcast_to(b2_ref[...], (LANES, nvars)).T
    loads[2].wait()
    loads[3].wait()
    loads[4].wait()
    loads[5].wait()

    def prepare(i, total):
        rows = pl.ds(pl.multiple_of(i * ROWS, ROWS), ROWS)
        masks = cut(mask_v[rows, 0, :].astype(jnp.float32), chunks, useful, halo)
        seen = cut(obs_v[rows, 0, :], chunks, useful, halo)
        for c in range(chunks):
            inn[0, c, rows] = masks[c]
            inn[1, c, rows] = seen[c]
        noise = noise_v[rows, 0, :]
        return total + jnp.sum(noise * noise)

    zsq = lax.fori_loop(0, nvars // ROWS, prepare, jnp.float32(0))
    gacc[...] = jnp.zeros_like(gacc)

    def taps(step, slot):
        x = win[step, slot]
        xf = x.astype(jnp.float32)
        left = pltpu.roll(xf, 1, 1).astype(jnp.bfloat16)
        right = pltpu.roll(xf, width - 1, 1).astype(jnp.bfloat16)
        stacked = jnp.concatenate([left, x, right], axis=0)
        return jnp.dot(w1t[slot], stacked, preferred_element_type=jnp.float32)

    lane = lax.broadcasted_iota(jnp.int32, (nvars, width), 1)
    valid = jnp.logical_and(lane >= halo, lane < halo + useful)

    @pl.loop(0, steps + 2)
    def _(turn):
        @pl.when(turn < steps)
        def _():
            direct(turn).wait_recv()

            @pl.when(has_onward)
            def _():
                forward(turn).start()

            @pl.when(core == par)
            def _():
                relay_to_sib(turn).start()

        @pl.when(jnp.logical_and(has_far, jnp.logical_and(turn >= 1, turn <= steps)))
        def _():
            forward(turn - 1).wait_recv()

            @pl.when(core != par)
            def _():
                relay_to_sib(turn - 1).start()

        @pl.when(turn >= 2)
        def _():
            step = turn - 2
            c = lax.rem(step, chunks)
            own_to_sib(step).wait_recv()
            pre = b1t[:, :1] + taps(step, 2) + taps(step, near) + taps(step, far) + taps(step, 3 - 2 * core)

            @pl.when(jnp.logical_or(core != par, has_far))
            def _():
                relay_to_sib(step).wait_recv()

            pre = pre + taps(step, 1 + 2 * core)
            hidden = (0.5 * pre * (1.0 + jnp.tanh(0.5 * pre))).astype(jnp.bfloat16)
            y = jnp.dot(w2_v[...].reshape(3 * nvars, hid), hidden, preferred_element_type=jnp.float32)
            out = pltpu.roll(y[:nvars], 1, 1) + y[nvars : 2 * nvars] + pltpu.roll(y[2 * nvars :], width - 1, 1)
            field = fld[c]
            score = out + b2t[:, :1] + inn[0, c] * (inn[1, c] - field)

            @pl.when(step < chunks)
            def _():
                moved = field + 0.5 * score
                fld[c] = moved
                win[step + chunks, 2] = moved.astype(jnp.bfloat16)
                direct(step + chunks).start()
                own_to_sib(step + chunks).start()

            @pl.when(step >= chunks)
            def _():
                drift[c] = score
                gacc[...] += jnp.where(valid, score * score, 0.0)

    gsq = gacc[...]
    row = lax.broadcasted_iota(jnp.int32, (8, LANES), 0)
    sums[me] = jnp.where(row == 0, zsq, jnp.sum(gsq))

    def share(device, slot):
        return pltpu.make_async_remote_copy(
            src_ref=sums.at[me],
            dst_ref=sums.at[slot],
            send_sem=sum_send.at[device],
            recv_sem=sum_recv.at[slot],
            device_id=(group, device),
            device_id_type=pl.DeviceIdType.MESH,
        )

    @pl.loop(1, n)
    def _(d):
        share(lax.rem(me + d, n), me).start()

    @pl.loop(1, n)
    def _(d):
        other = lax.rem(me + d, n)
        share(other, other).wait_recv()

    tot = jnp.sum(sums[...], axis=0)
    zall = tot[0:1, 0:1]
    gall = tot[1:2, 0:1]
    size = 2.0 * 0.16 * 0.16 * zall / (gall + 1e-06)
    scale = jnp.sqrt(2.0 * size)

    @pl.loop(0, nvars // ROWS)
    def _(i):
        rows = pl.ds(pl.multiple_of(i * ROWS, ROWS), ROWS)
        for c in range(chunks):
            piece = fld[c, rows] + size * drift[c, rows]
            span = slice(c * useful, (c + 1) * useful)
            out_ref[rows, span] = piece[:, halo : halo + useful] + scale * noise_v[rows, 0, span]

    @pl.loop(1, n)
    def _(d):
        share(lax.rem(me + d, n), me).wait_send()

    @pl.loop(0, steps)
    def _(step):
        direct(step).wait_send()
        own_to_sib(step).wait_send()

        @pl.when(has_onward)
        def _():
            forward(step).wait_send()

        @pl.when(jnp.logical_or(core == par, has_far))
        def _():
            relay_to_sib(step).wait_send()


def on_device(n, state, observed, obs_mask, noise, w_first, b_first, w_second, b_second):
    hours, nvars, lat, lon = state.shape
    hid = w_first.shape[0]
    assert hours == 1 and lat == 1 and n % 4 == 0
    assert w_first.shape[1:] == (5 * nvars, 3, 3)
    chunks = CHUNKS
    padded = -(-(lon + 8 * chunks) // (LANES * chunks)) * LANES * chunks
    width = padded // chunks
    assert lon % chunks == 0
    useful = lon // chunks
    halo = (width - useful) // 2
    assert halo >= 4 and useful + 2 * halo == width and halo <= useful
    flat = lambda a: a.reshape(nvars, 1, lon)
    any_spec = pl.BlockSpec(memory_space=pl.ANY)
    vmem = pl.BlockSpec(memory_space=pltpu.VMEM)
    steps = 2 * chunks
    flops = 4 * width * chunks * hid * nvars * (15 + 3)
    out = pl.pallas_call(
        functools.partial(kernel, n, chunks, useful, halo),
        out_shape=jax.ShapeDtypeStruct((nvars, lon), jnp.float32),
        in_specs=[any_spec] * 5 + [vmem, any_spec, vmem],
        out_specs=vmem,
        scratch_shapes=[
            pltpu.VMEM((nvars, 1, lon), jnp.float32),
            pltpu.VMEM((nvars, 1, lon), jnp.float32),
            pltpu.VMEM((nvars, 1, lon), jnp.int32),
            pltpu.VMEM((nvars, 1, lon), jnp.float32),
            pltpu.VMEM((3, 5 * nvars, hid), jnp.bfloat16),
            pltpu.VMEM((3, nvars, hid), jnp.bfloat16),
            pltpu.VMEM((5, hid, 3 * nvars), jnp.bfloat16),
            pltpu.VMEM((hid, LANES), jnp.float32),
            pltpu.VMEM((nvars, LANES), jnp.float32),
            pltpu.VMEM((chunks, nvars, width), jnp.float32),
            pltpu.VMEM((2, chunks, nvars, width), jnp.float32),
            pltpu.VMEM((chunks, nvars, width), jnp.float32),
            pltpu.VMEM((nvars, width), jnp.float32),
            pltpu.VMEM((steps, 5, nvars, width), jnp.bfloat16),
            pltpu.VMEM((n, 8, LANES), jnp.float32),
            pltpu.SemaphoreType.DMA((6,)),
            pltpu.SemaphoreType.DMA((steps, 4)),
            pltpu.SemaphoreType.DMA((steps, 4)),
            pltpu.SemaphoreType.DMA((n,)),
            pltpu.SemaphoreType.DMA((n,)),
        ],
        compiler_params=pltpu.CompilerParams(
            collective_id=0, has_side_effects=True, vmem_limit_bytes=62 * 1024 * 1024
        ),
        cost_estimate=pl.CostEstimate(flops=flops, bytes_accessed=4 * 1024 * 1024, transcendentals=0),
    )(
        flat(state),
        flat(observed),
        flat(obs_mask),
        flat(noise),
        jnp.transpose(w_first, (2, 3, 1, 0)),
        b_first.reshape(1, hid),
        jnp.transpose(w_second, (2, 3, 0, 1)),
        b_second.reshape(1, nvars),
    )
    return out.reshape(state.shape)


def solution(mesh):
    part = P(("groups", "tm"), None, None, None)
    return jax.shard_map(
        functools.partial(on_device, mesh.shape["tm"]),
        mesh=mesh,
        in_specs=(part, part, part, part, P(), P(), P(), P()),
        out_specs=part,
        check_vma=False,
    )
```

```python
import functools

import jax
import jax.numpy as jnp
from jax import lax
from jax.experimental import pallas as pl
from jax.experimental.pallas import tpu as pltpu
from jax.sharding import PartitionSpec as P

CHUNKS = 6
LANES = 128
ROWS = 16


def cut(field, chunks, useful, halo):
    lon = field.shape[-1]
    pieces = []
    for c in range(chunks):
        lo, hi = c * useful - halo, (c + 1) * useful + halo
        parts = []
        if lo < 0:
            parts.append(field[:, lon + lo :])
        parts.append(field[:, max(lo, 0) : min(hi, lon)])
        if hi > lon:
            parts.append(field[:, : hi - lon])
        pieces.append(jnp.concatenate(parts, axis=1) if len(parts) > 1 else parts[0])
    return pieces


def kernel(
    n, chunks, useful, halo,
    state_hbm, obs_hbm, mask_hbm, noise_hbm, w1_hbm, b1_ref, w2_hbm, b2_ref, out_ref,
    state_v, obs_v, mask_v, noise_v, w1_v, w2_v,
    w1t, b1t, b2t, fld, inn, drift, gacc, win, sums,
    local_sem, send_sem, recv_sem, sum_send, sum_recv,
):
    me = lax.axis_index("tm")
    group = lax.axis_index("groups")
    core = lax.rem(me, 2)
    par = lax.rem(me // 2, 2)
    sib = me + 1 - 2 * core
    partner = me + 2 - 4 * par
    onward = me + 4 - 8 * par
    near, far = 4 - 4 * par, 4 * par
    cousin = jnp.where(core == par, sib, onward + 1 - 2 * core)
    has_far = jnp.logical_or(jnp.logical_and(par == 0, me >= 4), jnp.logical_and(par == 1, me + 4 < n))
    has_onward = jnp.logical_or(jnp.logical_and(par == 0, me + 4 < n), jnp.logical_and(par == 1, me >= 4))
    has_cousin = jnp.logical_or(core == par, has_onward)
    nvars = fld.shape[1]
    hid = w1t.shape[1]
    width = fld.shape[2]
    steps = 2 * chunks

    barrier = pltpu.get_barrier_semaphore()

    @pl.loop(1, n)
    def _(d):
        pl.semaphore_signal(
            barrier, inc=1, device_id=(group, lax.rem(me + d, n)), device_id_type=pl.DeviceIdType.MESH
        )

    loads = []
    for i, (src, dst) in enumerate(
        (
            (state_hbm, state_v),
            (w1_hbm.at[w1_hbm.shape[0] // 2], w1_v),
            (w2_hbm.at[w2_hbm.shape[0] // 2], w2_v),
            (obs_hbm, obs_v),
            (mask_hbm, mask_v),
            (noise_hbm, noise_v),
        )
    ):
        loads.append(pltpu.make_async_copy(src, dst, local_sem.at[i]))
        loads[-1].start()

    def remote(step, kind, src, dst, device):
        return pltpu.make_async_remote_copy(
            src_ref=win.at[step, src],
            dst_ref=win.at[step, dst],
            send_sem=send_sem.at[step, kind],
            recv_sem=recv_sem.at[step, kind],
            device_id=(group, device),
            device_id_type=pl.DeviceIdType.MESH,
        )

    def direct(step):
        return remote(step, 0, 2, far, partner)

    def forward(step):
        return remote(step, 1, near, far, onward)

    def own_to_sib(step):
        return remote(step, 2, 2, 1 + 2 * core, sib)

    def relay(step):
        return remote(step, 3, near, 3 - 2 * core, cousin)

    @pl.when(jnp.logical_not(has_far))
    def _():
        @pl.loop(0, steps)
        def _(step):
            win[step, far] = jnp.zeros((nvars, width), jnp.bfloat16)

    @pl.when(jnp.logical_and(jnp.logical_not(has_far), core == par))
    def _():
        @pl.loop(0, steps)
        def _(step):
            win[step, 1 + 2 * core] = jnp.zeros((nvars, width), jnp.bfloat16)

    loads[0].wait()

    @pl.loop(0, nvars // ROWS)
    def _(i):
        rows = pl.ds(pl.multiple_of(i * ROWS, ROWS), ROWS)
        for c, piece in enumerate(cut(state_v[rows, 0, :], chunks, useful, halo)):
            fld[c, rows] = piece
            win[c, 2, rows] = piece.astype(jnp.bfloat16)

    pl.semaphore_wait(barrier, n - 1)

    @pl.loop(0, chunks)
    def _(c):
        direct(c).start()
        own_to_sib(c).start()

    loads[1].wait()

    @pl.loop(0, 5)
    def _(slot):
        rows = pl.ds(pl.multiple_of(slot * nvars, nvars), nvars)
        stacked = jnp.concatenate([w1_v[tap, rows, :] for tap in range(3)], axis=0)
        w1t[slot] = stacked.astype(jnp.float32).T.astype(jnp.bfloat16)

    b1t[...] = jnp.broadcast_to(b1_ref[...], (LANES, hid)).T
    b2t[...] = jnp.broadcast_to(b2_ref[...], (LANES, nvars)).T
    loads[2].wait()
    loads[3].wait()
    loads[4].wait()
    loads[5].wait()

    def prepare(i, total):
        rows = pl.ds(pl.multiple_of(i * ROWS, ROWS), ROWS)
        masks = cut(mask_v[rows, 0, :].astype(jnp.float32), chunks, useful, halo)
        seen = cut(obs_v[rows, 0, :], chunks, useful, halo)
        for c in range(chunks):
            inn[0, c, rows] = masks[c]
            inn[1, c, rows] = seen[c]
        noise = noise_v[rows, 0, :]
        return total + jnp.sum(noise * noise)

    zsq = lax.fori_loop(0, nvars // ROWS, prepare, jnp.float32(0))
    gacc[...] = jnp.zeros_like(gacc)

    def taps(step, slot):
        x = win[step, slot]
        xf = x.astype(jnp.float32)
        left = pltpu.roll(xf, 1, 1).astype(jnp.bfloat16)
        right = pltpu.roll(xf, width - 1, 1).astype(jnp.bfloat16)
        stacked = jnp.concatenate([left, x, right], axis=0)
        return jnp.dot(w1t[slot], stacked, preferred_element_type=jnp.float32)

    lane = lax.broadcasted_iota(jnp.int32, (nvars, width), 1)
    valid = jnp.logical_and(lane >= halo, lane < halo + useful)

    @pl.loop(0, steps + 1)
    def _(turn):
        @pl.when(turn < steps)
        def _():
            direct(turn).wait_recv()

            @pl.when(has_cousin)
            def _():
                relay(turn).start()

            @pl.when(has_onward)
            def _():
                forward(turn).start()

        @pl.when(turn >= 1)
        def _():
            step = turn - 1
            c = lax.rem(step, chunks)
            pre = b1t[:, :1] + taps(step, 2) + taps(step, near)
            own_to_sib(step).wait_recv()
            pre = pre + taps(step, 3 - 2 * core)

            @pl.when(has_far)
            def _():
                forward(step).wait_recv()

            pre = pre + taps(step, far)

            @pl.when(jnp.logical_or(core != par, has_far))
            def _():
                relay(step).wait_recv()

            pre = pre + taps(step, 1 + 2 * core)
            hidden = (0.5 * pre * (1.0 + jnp.tanh(0.5 * pre))).astype(jnp.bfloat16)
            y = jnp.dot(w2_v[...].reshape(3 * nvars, hid), hidden, preferred_element_type=jnp.float32)
            out = pltpu.roll(y[:nvars], 1, 1) + y[nvars : 2 * nvars] + pltpu.roll(y[2 * nvars :], width - 1, 1)
            field = fld[c]
            score = out + b2t[:, :1] + inn[0, c] * (inn[1, c] - field)

            @pl.when(step < chunks)
            def _():
                moved = field + 0.5 * score
                fld[c] = moved
                win[step + chunks, 2] = moved.astype(jnp.bfloat16)
                direct(step + chunks).start()
                own_to_sib(step + chunks).start()

            @pl.when(step >= chunks)
            def _():
                drift[c] = score
                gacc[...] += jnp.where(valid, score * score, 0.0)

    gsq = gacc[...]
    row = lax.broadcasted_iota(jnp.int32, (8, LANES), 0)
    sums[me] = jnp.where(row == 0, zsq, jnp.sum(gsq))

    def share(device, slot):
        return pltpu.make_async_remote_copy(
            src_ref=sums.at[me],
            dst_ref=sums.at[slot],
            send_sem=sum_send.at[device],
            recv_sem=sum_recv.at[slot],
            device_id=(group, device),
            device_id_type=pl.DeviceIdType.MESH,
        )

    @pl.loop(1, n)
    def _(d):
        share(lax.rem(me + d, n), me).start()

    @pl.loop(1, n)
    def _(d):
        other = lax.rem(me + d, n)
        share(other, other).wait_recv()

    tot = jnp.sum(sums[...], axis=0)
    zall = tot[0:1, 0:1]
    gall = tot[1:2, 0:1]
    size = 2.0 * 0.16 * 0.16 * zall / (gall + 1e-06)
    scale = jnp.sqrt(2.0 * size)

    @pl.loop(0, nvars // ROWS)
    def _(i):
        rows = pl.ds(pl.multiple_of(i * ROWS, ROWS), ROWS)
        for c in range(chunks):
            piece = fld[c, rows] + size * drift[c, rows]
            span = slice(c * useful, (c + 1) * useful)
            out_ref[rows, 0, span] = piece[:, halo : halo + useful] + scale * noise_v[rows, 0, span]

    @pl.loop(1, n)
    def _(d):
        share(lax.rem(me + d, n), me).wait_send()

    @pl.loop(0, steps)
    def _(step):
        direct(step).wait_send()
        own_to_sib(step).wait_send()

        @pl.when(has_onward)
        def _():
            forward(step).wait_send()

        @pl.when(has_cousin)
        def _():
            relay(step).wait_send()


def on_device(n, state, observed, obs_mask, noise, w_first, b_first, w_second, b_second):
    hours, nvars, lat, lon = state.shape
    hid = w_first.shape[0]
    assert hours == 1 and lat == 1 and n % 4 == 0
    assert w_first.shape[1:] == (5 * nvars, 3, 3)
    chunks = CHUNKS
    padded = -(-(lon + 8 * chunks) // (LANES * chunks)) * LANES * chunks
    width = padded // chunks
    assert lon % chunks == 0
    useful = lon // chunks
    halo = (width - useful) // 2
    assert halo >= 4 and useful + 2 * halo == width and halo <= useful
    flat = lambda a: a.reshape(nvars, 1, lon)
    any_spec = pl.BlockSpec(memory_space=pl.ANY)
    vmem = pl.BlockSpec(memory_space=pltpu.VMEM)
    steps = 2 * chunks
    flops = 4 * width * chunks * hid * nvars * (15 + 3)
    out = pl.pallas_call(
        functools.partial(kernel, n, chunks, useful, halo),
        out_shape=jax.ShapeDtypeStruct((nvars, 1, lon), jnp.float32),
        in_specs=[any_spec] * 5 + [vmem, any_spec, vmem],
        out_specs=vmem,
        scratch_shapes=[
            pltpu.VMEM((nvars, 1, lon), jnp.float32),
            pltpu.VMEM((nvars, 1, lon), jnp.float32),
            pltpu.VMEM((nvars, 1, lon), jnp.int32),
            pltpu.VMEM((nvars, 1, lon), jnp.float32),
            pltpu.VMEM((3, 5 * nvars, hid), jnp.bfloat16),
            pltpu.VMEM((3, nvars, hid), jnp.bfloat16),
            pltpu.VMEM((5, hid, 3 * nvars), jnp.bfloat16),
            pltpu.VMEM((hid, LANES), jnp.float32),
            pltpu.VMEM((nvars, LANES), jnp.float32),
            pltpu.VMEM((chunks, nvars, width), jnp.float32),
            pltpu.VMEM((2, chunks, nvars, width), jnp.float32),
            pltpu.VMEM((chunks, nvars, width), jnp.float32),
            pltpu.VMEM((nvars, width), jnp.float32),
            pltpu.VMEM((steps, 5, nvars, width), jnp.bfloat16),
            pltpu.VMEM((n, 8, LANES), jnp.float32),
            pltpu.SemaphoreType.DMA((6,)),
            pltpu.SemaphoreType.DMA((steps, 4)),
            pltpu.SemaphoreType.DMA((steps, 4)),
            pltpu.SemaphoreType.DMA((n,)),
            pltpu.SemaphoreType.DMA((n,)),
        ],
        compiler_params=pltpu.CompilerParams(
            collective_id=0, has_side_effects=True, vmem_limit_bytes=62 * 1024 * 1024
        ),
        cost_estimate=pl.CostEstimate(flops=flops, bytes_accessed=4 * 1024 * 1024, transcendentals=0),
    )(
        flat(state),
        flat(observed),
        flat(obs_mask),
        flat(noise),
        jnp.transpose(w_first, (2, 3, 1, 0)),
        b_first.reshape(1, hid),
        jnp.transpose(w_second, (2, 3, 0, 1)),
        b_second.reshape(1, nvars),
    )
    return out.reshape(state.shape)


def solution(mesh):
    part = P(("groups", "tm"), None, None, None)
    return jax.shard_map(
        functools.partial(on_device, mesh.shape["tm"]),
        mesh=mesh,
        in_specs=(part, part, part, part, P(), P(), P(), P()),
        out_specs=part,
        check_vma=False,
    )
```

```python
import functools

import jax
import jax.numpy as jnp
from jax import lax
from jax.experimental import pallas as pl
from jax.experimental.pallas import tpu as pltpu
from jax.sharding import PartitionSpec as P

CHUNKS = 3
LANES = 128
ROWS = 16


def cut(field, chunks, useful, halo):
    lon = field.shape[-1]
    pieces = []
    for c in range(chunks):
        lo, hi = c * useful - halo, (c + 1) * useful + halo
        parts = []
        if lo < 0:
            parts.append(field[:, lon + lo :])
        parts.append(field[:, max(lo, 0) : min(hi, lon)])
        if hi > lon:
            parts.append(field[:, : hi - lon])
        pieces.append(jnp.concatenate(parts, axis=1) if len(parts) > 1 else parts[0])
    return pieces


def kernel(
    n, chunks, useful, halo,
    state_hbm, obs_hbm, mask_hbm, noise_hbm, w1_hbm, b1_ref, w2_hbm, b2_ref, out_ref,
    state_v, obs_v, mask_v, noise_v, w1_v, w2_v,
    w1t, b1t, b2t, fld, inn, drift, gacc, win, sums,
    local_sem, send_sem, recv_sem, sum_send, sum_recv,
):
    me = lax.axis_index("tm")
    group = lax.axis_index("groups")
    core = lax.rem(me, 2)
    par = lax.rem(me // 2, 2)
    sib = me + 1 - 2 * core
    partner = me + 2 - 4 * par
    onward = me + 4 - 8 * par
    near, far = 4 - 4 * par, 4 * par
    cousin = jnp.where(core == par, sib, onward + 1 - 2 * core)
    has_far = jnp.logical_or(jnp.logical_and(par == 0, me >= 4), jnp.logical_and(par == 1, me + 4 < n))
    has_onward = jnp.logical_or(jnp.logical_and(par == 0, me + 4 < n), jnp.logical_and(par == 1, me >= 4))
    has_cousin = jnp.logical_or(core == par, has_onward)
    nvars = fld.shape[1]
    hid = w1t.shape[0]
    width = fld.shape[2]
    steps = 2 * chunks

    barrier = pltpu.get_barrier_semaphore()

    @pl.loop(1, n)
    def _(d):
        pl.semaphore_signal(
            barrier, inc=1, device_id=(group, lax.rem(me + d, n)), device_id_type=pl.DeviceIdType.MESH
        )

    loads = []
    for i, (src, dst) in enumerate(
        (
            (state_hbm, state_v),
            (w1_hbm.at[w1_hbm.shape[0] // 2], w1_v),
            (w2_hbm.at[w2_hbm.shape[0] // 2], w2_v),
            (obs_hbm, obs_v),
            (mask_hbm, mask_v),
            (noise_hbm, noise_v),
        )
    ):
        loads.append(pltpu.make_async_copy(src, dst, local_sem.at[i]))
        loads[-1].start()

    def remote(step, kind, src, dst, device):
        return pltpu.make_async_remote_copy(
            src_ref=win.at[step, src],
            dst_ref=win.at[step, dst],
            send_sem=send_sem.at[step, kind],
            recv_sem=recv_sem.at[step, kind],
            device_id=(group, device),
            device_id_type=pl.DeviceIdType.MESH,
        )

    def direct(step):
        return remote(step, 0, 2, far, partner)

    def forward(step):
        return remote(step, 1, near, far, onward)

    def own_to_sib(step):
        return remote(step, 2, 2, 1 + 2 * core, sib)

    def relay(step):
        return remote(step, 3, near, 3 - 2 * core, cousin)

    @pl.when(jnp.logical_not(has_far))
    def _():
        @pl.loop(0, steps)
        def _(step):
            win[step, far] = jnp.zeros((nvars, width), jnp.bfloat16)

    @pl.when(jnp.logical_and(jnp.logical_not(has_far), core == par))
    def _():
        @pl.loop(0, steps)
        def _(step):
            win[step, 1 + 2 * core] = jnp.zeros((nvars, width), jnp.bfloat16)

    loads[0].wait()

    @pl.loop(0, nvars // ROWS)
    def _(i):
        rows = pl.ds(pl.multiple_of(i * ROWS, ROWS), ROWS)
        for c, piece in enumerate(cut(state_v[rows, 0, :], chunks, useful, halo)):
            fld[c, rows] = piece
            win[c, 2, rows] = piece.astype(jnp.bfloat16)

    pl.semaphore_wait(barrier, n - 1)

    @pl.loop(0, chunks)
    def _(c):
        direct(c).start()
        own_to_sib(c).start()

    loads[1].wait()

    for slot in range(5):
        rows = slice(slot * nvars, (slot + 1) * nvars)
        stacked = jnp.concatenate([w1_v[tap, rows, :] for tap in range(3)], axis=0)
        w1t[:, slot * 3 * nvars : (slot + 1) * 3 * nvars] = stacked.astype(jnp.float32).T.astype(jnp.bfloat16)

    b1t[...] = jnp.broadcast_to(b1_ref[...], (LANES, hid)).T
    b2t[...] = jnp.broadcast_to(b2_ref[...], (LANES, nvars)).T
    loads[2].wait()
    loads[3].wait()
    loads[4].wait()
    loads[5].wait()

    def prepare(i, total):
        rows = pl.ds(pl.multiple_of(i * ROWS, ROWS), ROWS)
        masks = cut(mask_v[rows, 0, :].astype(jnp.float32), chunks, useful, halo)
        seen = cut(obs_v[rows, 0, :], chunks, useful, halo)
        for c in range(chunks):
            inn[0, c, rows] = masks[c]
            inn[1, c, rows] = seen[c]
        noise = noise_v[rows, 0, :]
        return total + jnp.sum(noise * noise)

    zsq = lax.fori_loop(0, nvars // ROWS, prepare, jnp.float32(0))
    gacc[...] = jnp.zeros_like(gacc)

    def taps(step, slot):
        x = win[step, slot]
        xf = x.astype(jnp.float32)
        return [pltpu.roll(xf, 1, 1).astype(jnp.bfloat16), x, pltpu.roll(xf, width - 1, 1).astype(jnp.bfloat16)]

    lane = lax.broadcasted_iota(jnp.int32, (nvars, width), 1)
    valid = jnp.logical_and(lane >= halo, lane < halo + useful)

    @pl.loop(0, steps + 1)
    def _(turn):
        @pl.when(turn < steps)
        def _():
            direct(turn).wait_recv()

            @pl.when(has_cousin)
            def _():
                relay(turn).start()

            @pl.when(has_onward)
            def _():
                forward(turn).start()

        @pl.when(turn >= 1)
        def _():
            step = turn - 1
            c = lax.rem(step, chunks)
            own_to_sib(step).wait_recv()

            @pl.when(has_far)
            def _():
                forward(step).wait_recv()

            @pl.when(jnp.logical_or(core != par, has_far))
            def _():
                relay(step).wait_recv()

            stacked = jnp.concatenate([row for slot in range(5) for row in taps(step, slot)], axis=0)
            pre = jnp.dot(w1t[...], stacked, preferred_element_type=jnp.float32) + b1t[:, :1]
            hidden = (0.5 * pre * (1.0 + jnp.tanh(0.5 * pre))).astype(jnp.bfloat16)
            y = jnp.dot(w2_v[...].reshape(3 * nvars, hid), hidden, preferred_element_type=jnp.float32)
            out = pltpu.roll(y[:nvars], 1, 1) + y[nvars : 2 * nvars] + pltpu.roll(y[2 * nvars :], width - 1, 1)
            field = fld[c]
            score = out + b2t[:, :1] + inn[0, c] * (inn[1, c] - field)

            @pl.when(step < chunks)
            def _():
                moved = field + 0.5 * score
                fld[c] = moved
                win[step + chunks, 2] = moved.astype(jnp.bfloat16)
                direct(step + chunks).start()
                own_to_sib(step + chunks).start()

            @pl.when(step >= chunks)
            def _():
                drift[c] = score
                gacc[...] += jnp.where(valid, score * score, 0.0)

    gsq = gacc[...]
    row = lax.broadcasted_iota(jnp.int32, (8, LANES), 0)
    sums[me] = jnp.where(row == 0, zsq, jnp.sum(gsq))

    def share(device, slot):
        return pltpu.make_async_remote_copy(
            src_ref=sums.at[me],
            dst_ref=sums.at[slot],
            send_sem=sum_send.at[device],
            recv_sem=sum_recv.at[slot],
            device_id=(group, device),
            device_id_type=pl.DeviceIdType.MESH,
        )

    @pl.loop(1, n)
    def _(d):
        share(lax.rem(me + d, n), me).start()

    @pl.loop(1, n)
    def _(d):
        other = lax.rem(me + d, n)
        share(other, other).wait_recv()

    tot = jnp.sum(sums[...], axis=0)
    zall = tot[0:1, 0:1]
    gall = tot[1:2, 0:1]
    size = 2.0 * 0.16 * 0.16 * zall / (gall + 1e-06)
    scale = jnp.sqrt(2.0 * size)

    @pl.loop(0, nvars // ROWS)
    def _(i):
        rows = pl.ds(pl.multiple_of(i * ROWS, ROWS), ROWS)
        for c in range(chunks):
            piece = fld[c, rows] + size * drift[c, rows]
            span = slice(c * useful, (c + 1) * useful)
            out_ref[rows, 0, span] = piece[:, halo : halo + useful] + scale * noise_v[rows, 0, span]

    @pl.loop(1, n)
    def _(d):
        share(lax.rem(me + d, n), me).wait_send()

    @pl.loop(0, steps)
    def _(step):
        direct(step).wait_send()
        own_to_sib(step).wait_send()

        @pl.when(has_onward)
        def _():
            forward(step).wait_send()

        @pl.when(has_cousin)
        def _():
            relay(step).wait_send()


def on_device(n, state, observed, obs_mask, noise, w_first, b_first, w_second, b_second):
    hours, nvars, lat, lon = state.shape
    hid = w_first.shape[0]
    assert hours == 1 and lat == 1 and n % 4 == 0
    assert w_first.shape[1:] == (5 * nvars, 3, 3)
    chunks = CHUNKS
    padded = -(-(lon + 8 * chunks) // (LANES * chunks)) * LANES * chunks
    width = padded // chunks
    assert lon % chunks == 0
    useful = lon // chunks
    halo = (width - useful) // 2
    assert halo >= 4 and useful + 2 * halo == width and halo <= useful
    flat = lambda a: a.reshape(nvars, 1, lon)
    any_spec = pl.BlockSpec(memory_space=pl.ANY)
    vmem = pl.BlockSpec(memory_space=pltpu.VMEM)
    steps = 2 * chunks
    flops = 4 * width * chunks * hid * nvars * (15 + 3)
    out = pl.pallas_call(
        functools.partial(kernel, n, chunks, useful, halo),
        out_shape=jax.ShapeDtypeStruct((nvars, 1, lon), jnp.float32),
        in_specs=[any_spec] * 5 + [vmem, any_spec, vmem],
        out_specs=vmem,
        scratch_shapes=[
            pltpu.VMEM((nvars, 1, lon), jnp.float32),
            pltpu.VMEM((nvars, 1, lon), jnp.float32),
            pltpu.VMEM((nvars, 1, lon), jnp.int32),
            pltpu.VMEM((nvars, 1, lon), jnp.float32),
            pltpu.VMEM((3, 5 * nvars, hid), jnp.bfloat16),
            pltpu.VMEM((3, nvars, hid), jnp.bfloat16),
            pltpu.VMEM((hid, 15 * nvars), jnp.bfloat16),
            pltpu.VMEM((hid, LANES), jnp.float32),
            pltpu.VMEM((nvars, LANES), jnp.float32),
            pltpu.VMEM((chunks, nvars, width), jnp.float32),
            pltpu.VMEM((2, chunks, nvars, width), jnp.float32),
            pltpu.VMEM((chunks, nvars, width), jnp.float32),
            pltpu.VMEM((nvars, width), jnp.float32),
            pltpu.VMEM((steps, 5, nvars, width), jnp.bfloat16),
            pltpu.VMEM((n, 8, LANES), jnp.float32),
            pltpu.SemaphoreType.DMA((6,)),
            pltpu.SemaphoreType.DMA((steps, 4)),
            pltpu.SemaphoreType.DMA((steps, 4)),
            pltpu.SemaphoreType.DMA((n,)),
            pltpu.SemaphoreType.DMA((n,)),
        ],
        compiler_params=pltpu.CompilerParams(
            collective_id=0, has_side_effects=True, vmem_limit_bytes=62 * 1024 * 1024
        ),
        cost_estimate=pl.CostEstimate(flops=flops, bytes_accessed=4 * 1024 * 1024, transcendentals=0),
    )(
        flat(state),
        flat(observed),
        flat(obs_mask),
        flat(noise),
        jnp.transpose(w_first, (2, 3, 1, 0)),
        b_first.reshape(1, hid),
        jnp.transpose(w_second, (2, 3, 0, 1)),
        b_second.reshape(1, nvars),
    )
    return out.reshape(state.shape)


def solution(mesh):
    part = P(("groups", "tm"), None, None, None)
    return jax.shard_map(
        functools.partial(on_device, mesh.shape["tm"]),
        mesh=mesh,
        in_specs=(part, part, part, part, P(), P(), P(), P()),
        out_specs=part,
        check_vma=False,
    )
```

```python
import functools

import jax
import jax.numpy as jnp
from jax import lax
from jax.experimental import pallas as pl
from jax.experimental.pallas import tpu as pltpu
from jax.sharding import PartitionSpec as P

CHUNKS = 3
LANES = 128
ROWS = 16


def cut(field, chunks, useful, halo):
    lon = field.shape[-1]
    pieces = []
    for c in range(chunks):
        lo, hi = c * useful - halo, (c + 1) * useful + halo
        parts = []
        if lo < 0:
            parts.append(field[:, lon + lo :])
        parts.append(field[:, max(lo, 0) : min(hi, lon)])
        if hi > lon:
            parts.append(field[:, : hi - lon])
        pieces.append(jnp.concatenate(parts, axis=1) if len(parts) > 1 else parts[0])
    return pieces


def kernel(
    n, chunks, useful, halo,
    state_hbm, obs_hbm, mask_hbm, noise_hbm, w1_hbm, b1_ref, w2_hbm, b2_ref, out_ref,
    state_v, obs_v, mask_v, noise_v, w1_v, w2_v,
    w1t, b1t, b2t, fld, inn, drift, gacc, acc, whole, win, sums,
    local_sem, send_sem, recv_sem, sum_send, sum_recv,
):
    me = lax.axis_index("tm")
    group = lax.axis_index("groups")
    core = lax.rem(me, 2)
    par = lax.rem(me // 2, 2)
    sib = me + 1 - 2 * core
    partner = me + 2 - 4 * par
    onward = me + 4 - 8 * par
    near, far = 4 - 4 * par, 4 * par
    cousin = jnp.where(core == par, sib, onward + 1 - 2 * core)
    has_far = jnp.logical_or(jnp.logical_and(par == 0, me >= 4), jnp.logical_and(par == 1, me + 4 < n))
    has_onward = jnp.logical_or(jnp.logical_and(par == 0, me + 4 < n), jnp.logical_and(par == 1, me >= 4))
    has_cousin = jnp.logical_or(core == par, has_onward)
    nvars = fld.shape[1]
    hid = w1t.shape[0]
    width = fld.shape[2]
    steps = 2 * chunks

    barrier = pltpu.get_barrier_semaphore()

    loads = []
    for i, (src, dst) in enumerate(
        (
            (state_hbm, state_v),
            (w1_hbm.at[w1_hbm.shape[0] // 2], w1_v),
            (w2_hbm.at[w2_hbm.shape[0] // 2], w2_v),
            (obs_hbm, obs_v),
            (mask_hbm, mask_v),
            (noise_hbm, noise_v),
        )
    ):
        loads.append(pltpu.make_async_copy(src, dst, local_sem.at[i]))
        loads[-1].start()

    @pl.loop(1, n)
    def _(d):
        pl.semaphore_signal(
            barrier, inc=1, device_id=(group, lax.rem(me + d, n)), device_id_type=pl.DeviceIdType.MESH
        )

    def remote(step, kind, src, dst, device):
        return pltpu.make_async_remote_copy(
            src_ref=win.at[step, src],
            dst_ref=win.at[step, dst],
            send_sem=send_sem.at[step, kind],
            recv_sem=recv_sem.at[step, kind],
            device_id=(group, device),
            device_id_type=pl.DeviceIdType.MESH,
        )

    def direct(step):
        return remote(step, 0, 2, far, partner)

    def forward(step):
        return remote(step, 1, near, far, onward)

    def own_to_sib(step):
        return remote(step, 2, 2, 1 + 2 * core, sib)

    def relay(step):
        return remote(step, 3, near, 3 - 2 * core, cousin)

    @pl.when(jnp.logical_not(has_far))
    def _():
        @pl.loop(0, steps)
        def _(step):
            win[step, far] = jnp.zeros((nvars, width), jnp.bfloat16)

    @pl.when(jnp.logical_and(jnp.logical_not(has_far), core == par))
    def _():
        @pl.loop(0, steps)
        def _(step):
            win[step, 1 + 2 * core] = jnp.zeros((nvars, width), jnp.bfloat16)

    loads[0].wait()

    @pl.loop(0, nvars // ROWS)
    def _(i):
        rows = pl.ds(pl.multiple_of(i * ROWS, ROWS), ROWS)
        for c, piece in enumerate(cut(state_v[rows, 0, :], chunks, useful, halo)):
            fld[c, rows] = piece
            win[c, 2, rows] = piece.astype(jnp.bfloat16)

    pl.semaphore_wait(barrier, n - 1)

    @pl.loop(0, chunks)
    def _(c):
        direct(c).start()
        own_to_sib(c).start()

    loads[1].wait()

    roles = (2, 3 - 2 * core, near, far, 1 + 2 * core)
    for role, slot in enumerate(roles):
        rows = pl.ds(pl.multiple_of(slot * nvars, nvars), nvars)
        stacked = jnp.concatenate([w1_v[tap, rows, :] for tap in range(3)], axis=0)
        w1t[:, role * 3 * nvars : (role + 1) * 3 * nvars] = stacked.astype(jnp.float32).T.astype(jnp.bfloat16)

    b1t[...] = jnp.broadcast_to(b1_ref[...], (LANES, hid)).T
    b2t[...] = jnp.broadcast_to(b2_ref[...], (LANES, nvars)).T
    loads[2].wait()
    loads[3].wait()
    loads[4].wait()
    loads[5].wait()

    def prepare(i, total):
        rows = pl.ds(pl.multiple_of(i * ROWS, ROWS), ROWS)
        masks = cut(mask_v[rows, 0, :].astype(jnp.float32), chunks, useful, halo)
        seen = cut(obs_v[rows, 0, :], chunks, useful, halo)
        for c in range(chunks):
            inn[0, c, rows] = masks[c]
            inn[1, c, rows] = seen[c]
        noise = noise_v[rows, 0, :]
        whole[2, rows] = noise
        return total + jnp.sum(noise * noise)

    zsq = lax.fori_loop(0, nvars // ROWS, prepare, jnp.float32(0))
    gacc[...] = jnp.zeros_like(gacc)

    def taps(step, slot):
        x = win[step, slot]
        xf = x.astype(jnp.float32)
        return [pltpu.roll(xf, 1, 1).astype(jnp.bfloat16), x, pltpu.roll(xf, width - 1, 1).astype(jnp.bfloat16)]

    split = 2 * 3 * nvars

    def product(step, first, last, weights):
        stacked = jnp.concatenate([row for role in range(first, last) for row in taps(step, roles[role])], axis=0)
        return jnp.dot(weights, stacked, preferred_element_type=jnp.float32)

    def begin(step, c):
        own_to_sib(step).wait_recv()
        acc[c] = product(step, 0, 2, w1t[:, :split]) + b1t[:, :1]

    @pl.loop(0, chunks)
    def _(c):
        begin(c, c)

    lane = lax.broadcasted_iota(jnp.int32, (nvars, width), 1)
    valid = jnp.logical_and(lane >= halo, lane < halo + useful)

    @pl.loop(0, steps + 1)
    def _(turn):
        @pl.when(turn < steps)
        def _():
            direct(turn).wait_recv()

            @pl.when(has_cousin)
            def _():
                relay(turn).start()

            @pl.when(has_onward)
            def _():
                forward(turn).start()

        @pl.when(turn >= 1)
        def _():
            step = turn - 1
            c = lax.rem(step, chunks)

            @pl.when(step >= chunks)
            def _():
                begin(step, c)

            @pl.when(has_far)
            def _():
                forward(step).wait_recv()

            @pl.when(jnp.logical_or(core != par, has_far))
            def _():
                relay(step).wait_recv()

            pre = acc[c] + product(step, 2, 5, w1t[:, split:])
            hidden = (0.5 * pre * (1.0 + jnp.tanh(0.5 * pre))).astype(jnp.bfloat16)
            y = jnp.dot(w2_v[...].reshape(3 * nvars, hid), hidden, preferred_element_type=jnp.float32)
            out = pltpu.roll(y[:nvars], 1, 1) + y[nvars : 2 * nvars] + pltpu.roll(y[2 * nvars :], width - 1, 1)
            field = fld[c]
            score = out + b2t[:, :1] + inn[0, c] * (inn[1, c] - field)

            @pl.when(step < chunks)
            def _():
                moved = field + 0.5 * score
                fld[c] = moved
                win[step + chunks, 2] = moved.astype(jnp.bfloat16)
                direct(step + chunks).start()
                own_to_sib(step + chunks).start()

            @pl.when(step >= chunks)
            def _():
                drift[c] = score
                gacc[...] += jnp.where(valid, score * score, 0.0)

    gsq = gacc[...]
    row = lax.broadcasted_iota(jnp.int32, (8, LANES), 0)
    sums[me] = jnp.where(row == 0, zsq, jnp.sum(gsq))

    def share(device, slot):
        return pltpu.make_async_remote_copy(
            src_ref=sums.at[me],
            dst_ref=sums.at[slot],
            send_sem=sum_send.at[device],
            recv_sem=sum_recv.at[slot],
            device_id=(group, device),
            device_id_type=pl.DeviceIdType.MESH,
        )

    @pl.loop(1, n)
    def _(d):
        share(lax.rem(me + d, n), me).start()

    @pl.loop(0, nvars // ROWS)
    def _(i):
        rows = pl.ds(pl.multiple_of(i * ROWS, ROWS), ROWS)
        for c in range(chunks):
            span = slice(c * useful, (c + 1) * useful)
            whole[0, rows, span] = fld[c, rows, halo : halo + useful]
            whole[1, rows, span] = drift[c, rows, halo : halo + useful]

    @pl.loop(1, n)
    def _(d):
        other = lax.rem(me + d, n)
        share(other, other).wait_recv()

    tot = jnp.sum(sums[...], axis=0)
    zall = tot[0:1, 0:1]
    gall = tot[1:2, 0:1]
    size = 2.0 * 0.16 * 0.16 * zall / (gall + 1e-06)
    scale = jnp.sqrt(2.0 * size)

    @pl.loop(0, nvars // ROWS)
    def _(i):
        rows = pl.ds(pl.multiple_of(i * ROWS, ROWS), ROWS)
        out_ref[rows, 0, :] = whole[0, rows] + size * whole[1, rows] + scale * whole[2, rows]

    @pl.loop(1, n)
    def _(d):
        share(lax.rem(me + d, n), me).wait_send()

    @pl.loop(0, steps)
    def _(step):
        direct(step).wait_send()
        own_to_sib(step).wait_send()

        @pl.when(has_onward)
        def _():
            forward(step).wait_send()

        @pl.when(has_cousin)
        def _():
            relay(step).wait_send()


def on_device(n, state, observed, obs_mask, noise, w_first, b_first, w_second, b_second):
    hours, nvars, lat, lon = state.shape
    hid = w_first.shape[0]
    assert hours == 1 and lat == 1 and n % 4 == 0
    assert w_first.shape[1:] == (5 * nvars, 3, 3)
    chunks = CHUNKS
    padded = -(-(lon + 8 * chunks) // (LANES * chunks)) * LANES * chunks
    width = padded // chunks
    assert lon % chunks == 0
    useful = lon // chunks
    halo = (width - useful) // 2
    assert halo >= 4 and useful + 2 * halo == width and halo <= useful
    flat = lambda a: a.reshape(nvars, 1, lon)
    any_spec = pl.BlockSpec(memory_space=pl.ANY)
    vmem = pl.BlockSpec(memory_space=pltpu.VMEM)
    steps = 2 * chunks
    flops = 4 * width * chunks * hid * nvars * (15 + 3)
    out = pl.pallas_call(
        functools.partial(kernel, n, chunks, useful, halo),
        out_shape=jax.ShapeDtypeStruct((nvars, 1, lon), jnp.float32),
        in_specs=[any_spec] * 5 + [vmem, any_spec, vmem],
        out_specs=vmem,
        scratch_shapes=[
            pltpu.VMEM((nvars, 1, lon), jnp.float32),
            pltpu.VMEM((nvars, 1, lon), jnp.float32),
            pltpu.VMEM((nvars, 1, lon), jnp.int32),
            pltpu.VMEM((nvars, 1, lon), jnp.float32),
            pltpu.VMEM((3, 5 * nvars, hid), jnp.bfloat16),
            pltpu.VMEM((3, nvars, hid), jnp.bfloat16),
            pltpu.VMEM((hid, 15 * nvars), jnp.bfloat16),
            pltpu.VMEM((hid, LANES), jnp.float32),
            pltpu.VMEM((nvars, LANES), jnp.float32),
            pltpu.VMEM((chunks, nvars, width), jnp.float32),
            pltpu.VMEM((2, chunks, nvars, width), jnp.float32),
            pltpu.VMEM((chunks, nvars, width), jnp.float32),
            pltpu.VMEM((nvars, width), jnp.float32),
            pltpu.VMEM((chunks, hid, width), jnp.float32),
            pltpu.VMEM((3, nvars, lon), jnp.float32),
            pltpu.VMEM((steps, 5, nvars, width), jnp.bfloat16),
            pltpu.VMEM((n, 8, LANES), jnp.float32),
            pltpu.SemaphoreType.DMA((6,)),
            pltpu.SemaphoreType.DMA((steps, 4)),
            pltpu.SemaphoreType.DMA((steps, 4)),
            pltpu.SemaphoreType.DMA((n,)),
            pltpu.SemaphoreType.DMA((n,)),
        ],
        compiler_params=pltpu.CompilerParams(
            collective_id=0, has_side_effects=True, vmem_limit_bytes=62 * 1024 * 1024
        ),
        cost_estimate=pl.CostEstimate(flops=flops, bytes_accessed=4 * 1024 * 1024, transcendentals=0),
    )(
        flat(state),
        flat(observed),
        flat(obs_mask),
        flat(noise),
        jnp.transpose(w_first, (2, 3, 1, 0)),
        b_first.reshape(1, hid),
        jnp.transpose(w_second, (2, 3, 0, 1)),
        b_second.reshape(1, nvars),
    )
    return out.reshape(state.shape)


def solution(mesh):
    part = P(("groups", "tm"), None, None, None)
    return jax.shard_map(
        functools.partial(on_device, mesh.shape["tm"]),
        mesh=mesh,
        in_specs=(part, part, part, part, P(), P(), P(), P()),
        out_specs=part,
        check_vma=False,
    )
```

```python
import functools
import math

import jax
import jax.numpy as jnp
from jax import lax
from jax.experimental import pallas as pl
from jax.experimental.pallas import tpu as pltpu
from jax.sharding import PartitionSpec as P

CHUNKS = 3
LANES = 128
ROWS = 16
RADIX = 4


def cut(field, chunks, useful, halo):
    lon = field.shape[-1]
    pieces = []
    for c in range(chunks):
        lo, hi = c * useful - halo, (c + 1) * useful + halo
        parts = []
        if lo < 0:
            parts.append(field[:, lon + lo :])
        parts.append(field[:, max(lo, 0) : min(hi, lon)])
        if hi > lon:
            parts.append(field[:, : hi - lon])
        pieces.append(jnp.concatenate(parts, axis=1) if len(parts) > 1 else parts[0])
    return pieces


def kernel(
    n, chunks, useful, halo,
    state_hbm, obs_hbm, mask_hbm, noise_hbm, w1_hbm, b1_ref, w2_hbm, b2_ref, out_ref,
    state_v, obs_v, mask_v, noise_v, w1_v, w2_v,
    w1t, b1t, b2t, fld, inn, drift, gacc, acc, whole, win, sums,
    local_sem, send_sem, recv_sem, sum_send, sum_recv,
):
    me = lax.axis_index("tm")
    group = lax.axis_index("groups")
    core = lax.rem(me, 2)
    par = lax.rem(me // 2, 2)
    sib = me + 1 - 2 * core
    partner = me + 2 - 4 * par
    onward = me + 4 - 8 * par
    source = me - 4 + 8 * par
    near, far = 4 - 4 * par, 4 * par
    cousin = jnp.where(core == par, sib, onward + 1 - 2 * core)
    has_far = jnp.logical_or(jnp.logical_and(par == 0, me >= 4), jnp.logical_and(par == 1, me + 4 < n))
    has_onward = jnp.logical_or(jnp.logical_and(par == 0, me + 4 < n), jnp.logical_and(par == 1, me >= 4))
    has_cousin = jnp.logical_or(core == par, has_onward)
    nvars = fld.shape[1]
    hid = w1t.shape[0]
    width = fld.shape[2]
    steps = 2 * chunks

    barrier = pltpu.get_barrier_semaphore()

    loads = []
    for i, (src, dst) in enumerate(
        (
            (state_hbm, state_v),
            (w1_hbm.at[w1_hbm.shape[0] // 2], w1_v),
            (w2_hbm.at[w2_hbm.shape[0] // 2], w2_v),
            (obs_hbm, obs_v),
            (mask_hbm, mask_v),
            (noise_hbm, noise_v),
        )
    ):
        loads.append(pltpu.make_async_copy(src, dst, local_sem.at[i]))
        loads[-1].start()

    strides = [RADIX**i for i in range(round(math.log(n, RADIX)))]

    def peer(stride, turn):
        digit = lax.rem(me // stride, RADIX)
        return me + (lax.rem(digit + turn, RADIX) - digit) * stride

    def greet(device):
        pl.semaphore_signal(barrier, inc=1, device_id=(group, device), device_id_type=pl.DeviceIdType.MESH)

    for stride in strides:
        for turn in range(1, RADIX):
            greet(peer(stride, turn))

    @pl.when(has_far)
    def _():
        greet(source)

        @pl.when(core == par)
        def _():
            greet(source + 1 - 2 * core)

    def remote(step, kind, src, dst, device):
        return pltpu.make_async_remote_copy(
            src_ref=win.at[step, src],
            dst_ref=win.at[step, dst],
            send_sem=send_sem.at[step, kind],
            recv_sem=recv_sem.at[step, kind],
            device_id=(group, device),
            device_id_type=pl.DeviceIdType.MESH,
        )

    def direct(step):
        return remote(step, 0, 2, far, partner)

    def forward(step):
        return remote(step, 1, near, far, onward)

    def own_to_sib(step):
        return remote(step, 2, 2, 1 + 2 * core, sib)

    def relay(step):
        return remote(step, 3, near, 3 - 2 * core, cousin)

    @pl.when(jnp.logical_not(has_far))
    def _():
        @pl.loop(0, steps)
        def _(step):
            win[step, far] = jnp.zeros((nvars, width), jnp.bfloat16)

    @pl.when(jnp.logical_and(jnp.logical_not(has_far), core == par))
    def _():
        @pl.loop(0, steps)
        def _(step):
            win[step, 1 + 2 * core] = jnp.zeros((nvars, width), jnp.bfloat16)

    loads[0].wait()

    @pl.loop(0, nvars // ROWS)
    def _(i):
        rows = pl.ds(pl.multiple_of(i * ROWS, ROWS), ROWS)
        for c, piece in enumerate(cut(state_v[rows, 0, :], chunks, useful, halo)):
            fld[c, rows] = piece
            win[c, 2, rows] = piece.astype(jnp.bfloat16)

    extra = jnp.where(has_onward, jnp.where(core == par, 1, 2), 0)
    pl.semaphore_wait(barrier, (RADIX - 1) * len(strides) + extra)

    @pl.loop(0, chunks)
    def _(c):
        direct(c).start()
        own_to_sib(c).start()

    def pass_on(step):
        direct(step).wait_recv()

        @pl.when(has_onward)
        def _():
            forward(step).start()

        @pl.when(has_cousin)
        def _():
            relay(step).start()

    loads[1].wait()

    roles = (2, 3 - 2 * core, near, far, 1 + 2 * core)
    for role, slot in enumerate(roles):
        rows = pl.ds(pl.multiple_of(slot * nvars, nvars), nvars)
        stacked = jnp.concatenate([w1_v[tap, rows, :] for tap in range(3)], axis=0)
        w1t[:, role * 3 * nvars : (role + 1) * 3 * nvars] = stacked.astype(jnp.float32).T.astype(jnp.bfloat16)

    pass_on(0)
    b1t[...] = jnp.broadcast_to(b1_ref[...], (LANES, hid)).T
    b2t[...] = jnp.broadcast_to(b2_ref[...], (LANES, nvars)).T
    loads[2].wait()
    loads[3].wait()
    loads[4].wait()
    loads[5].wait()

    def prepare(i, total):
        rows = pl.ds(pl.multiple_of(i * ROWS, ROWS), ROWS)
        masks = cut(mask_v[rows, 0, :].astype(jnp.float32), chunks, useful, halo)
        seen = cut(obs_v[rows, 0, :], chunks, useful, halo)
        for c in range(chunks):
            inn[0, c, rows] = masks[c]
            inn[1, c, rows] = seen[c]
        noise = noise_v[rows, 0, :]
        whole[2, rows] = noise
        return total + jnp.sum(noise * noise)

    zsq = lax.fori_loop(0, nvars // ROWS, prepare, jnp.float32(0))
    gacc[...] = jnp.zeros_like(gacc)

    def taps(step, slot):
        x = win[step, slot]
        xf = x.astype(jnp.float32)
        return [pltpu.roll(xf, 1, 1).astype(jnp.bfloat16), x, pltpu.roll(xf, width - 1, 1).astype(jnp.bfloat16)]

    lane = lax.broadcasted_iota(jnp.int32, (nvars, width), 1)
    valid = jnp.logical_and(lane >= halo, lane < halo + useful)
    split = 2 * 3 * nvars

    def product(step, first, last, weights):
        stacked = jnp.concatenate([row for role in range(first, last) for row in taps(step, roles[role])], axis=0)
        return jnp.dot(weights, stacked, preferred_element_type=jnp.float32)

    def begin(step, c):
        own_to_sib(step).wait_recv()
        acc[c] = product(step, 0, 2, w1t[:, :split]) + b1t[:, :1]

    def finish(step, c):
        @pl.when(has_far)
        def _():
            forward(step).wait_recv()

        @pl.when(jnp.logical_or(core != par, has_far))
        def _():
            relay(step).wait_recv()

        pre = acc[c] + product(step, 2, 5, w1t[:, split:])
        hidden = (0.5 * pre * (1.0 + jnp.tanh(0.5 * pre))).astype(jnp.bfloat16)
        y = jnp.dot(w2_v[...].reshape(3 * nvars, hid), hidden, preferred_element_type=jnp.float32)
        out = pltpu.roll(y[:nvars], 1, 1) + y[nvars : 2 * nvars] + pltpu.roll(y[2 * nvars :], width - 1, 1)
        field = fld[c]
        return field, out + b2t[:, :1] + inn[0, c] * (inn[1, c] - field)

    @pl.loop(1, chunks)
    def _(c):
        begin(c - 1, c - 1)
        pass_on(c)

    begin(chunks - 1, chunks - 1)

    @pl.loop(0, chunks)
    def _(c):
        field, score = finish(c, c)
        moved = field + 0.5 * score
        fld[c] = moved
        win[c + chunks, 2] = moved.astype(jnp.bfloat16)
        direct(c + chunks).start()
        own_to_sib(c + chunks).start()

        @pl.when(c >= 1)
        def _():
            pass_on(c + chunks - 1)

    @pl.loop(0, chunks - 1)
    def _(c):
        begin(c + chunks, c)

    pass_on(steps - 1)
    begin(steps - 1, chunks - 1)

    @pl.loop(0, chunks)
    def _(c):
        _, score = finish(c + chunks, c)
        drift[c] = score
        gacc[...] += jnp.where(valid, score * score, 0.0)

    gsq = gacc[...]
    def share(stage, turn):
        stride = strides[stage]
        return pltpu.make_async_remote_copy(
            src_ref=sums.at[stage, 0],
            dst_ref=sums.at[stage, turn],
            send_sem=sum_send.at[stage, turn],
            recv_sem=sum_recv.at[stage, turn],
            device_id=(group, peer(stride, turn)),
            device_id_type=pl.DeviceIdType.MESH,
        )

    row = lax.broadcasted_iota(jnp.int32, (8, LANES), 0)
    tot = jnp.where(row == 0, zsq, jnp.sum(gsq))
    for stage in range(len(strides)):
        sums[stage, 0] = tot
        for turn in range(1, RADIX):
            share(stage, turn).start()

        if stage == 0:

            @pl.loop(0, nvars // ROWS)
            def _(i):
                rows = pl.ds(pl.multiple_of(i * ROWS, ROWS), ROWS)
                for c in range(chunks):
                    span = slice(c * useful, (c + 1) * useful)
                    whole[0, rows, span] = fld[c, rows, halo : halo + useful]
                    whole[1, rows, span] = drift[c, rows, halo : halo + useful]

        for turn in range(1, RADIX):
            share(stage, turn).wait_recv()
        tot = (sums[stage, 0] + sums[stage, 2]) + (sums[stage, 1] + sums[stage, 3])

    zall = tot[0:1, 0:1]
    gall = tot[1:2, 0:1]
    size = 2.0 * 0.16 * 0.16 * zall / (gall + 1e-06)
    scale = jnp.sqrt(2.0 * size)

    @pl.loop(0, nvars // ROWS)
    def _(i):
        rows = pl.ds(pl.multiple_of(i * ROWS, ROWS), ROWS)
        out_ref[rows, 0, :] = whole[0, rows] + size * whole[1, rows] + scale * whole[2, rows]

    for stage in range(len(strides)):
        for turn in range(1, RADIX):
            share(stage, turn).wait_send()

    @pl.loop(0, steps)
    def _(step):
        direct(step).wait_send()
        own_to_sib(step).wait_send()

        @pl.when(has_onward)
        def _():
            forward(step).wait_send()

        @pl.when(has_cousin)
        def _():
            relay(step).wait_send()


def on_device(n, state, observed, obs_mask, noise, w_first, b_first, w_second, b_second):
    hours, nvars, lat, lon = state.shape
    hid = w_first.shape[0]
    assert hours == 1 and lat == 1 and n % 4 == 0
    assert w_first.shape[1:] == (5 * nvars, 3, 3)
    chunks = CHUNKS
    padded = -(-(lon + 8 * chunks) // (LANES * chunks)) * LANES * chunks
    width = padded // chunks
    assert lon % chunks == 0
    useful = lon // chunks
    halo = (width - useful) // 2
    assert halo >= 4 and useful + 2 * halo == width and halo <= useful
    flat = lambda a: a.reshape(nvars, 1, lon)
    any_spec = pl.BlockSpec(memory_space=pl.ANY)
    vmem = pl.BlockSpec(memory_space=pltpu.VMEM)
    steps = 2 * chunks
    stages = round(math.log(n, RADIX))
    assert RADIX**stages == n
    flops = 4 * width * chunks * hid * nvars * (15 + 3)
    out = pl.pallas_call(
        functools.partial(kernel, n, chunks, useful, halo),
        out_shape=jax.ShapeDtypeStruct((nvars, 1, lon), jnp.float32),
        in_specs=[any_spec] * 5 + [vmem, any_spec, vmem],
        out_specs=vmem,
        scratch_shapes=[
            pltpu.VMEM((nvars, 1, lon), jnp.float32),
            pltpu.VMEM((nvars, 1, lon), jnp.float32),
            pltpu.VMEM((nvars, 1, lon), jnp.int32),
            pltpu.VMEM((nvars, 1, lon), jnp.float32),
            pltpu.VMEM((3, 5 * nvars, hid), jnp.bfloat16),
            pltpu.VMEM((3, nvars, hid), jnp.bfloat16),
            pltpu.VMEM((hid, 15 * nvars), jnp.bfloat16),
            pltpu.VMEM((hid, LANES), jnp.float32),
            pltpu.VMEM((nvars, LANES), jnp.float32),
            pltpu.VMEM((chunks, nvars, width), jnp.float32),
            pltpu.VMEM((2, chunks, nvars, width), jnp.float32),
            pltpu.VMEM((chunks, nvars, width), jnp.float32),
            pltpu.VMEM((nvars, width), jnp.float32),
            pltpu.VMEM((chunks, hid, width), jnp.float32),
            pltpu.VMEM((3, nvars, lon), jnp.float32),
            pltpu.VMEM((steps, 5, nvars, width), jnp.bfloat16),
            pltpu.VMEM((stages, RADIX, 8, LANES), jnp.float32),
            pltpu.SemaphoreType.DMA((6,)),
            pltpu.SemaphoreType.DMA((steps, 4)),
            pltpu.SemaphoreType.DMA((steps, 4)),
            pltpu.SemaphoreType.DMA((stages, RADIX)),
            pltpu.SemaphoreType.DMA((stages, RADIX)),
        ],
        compiler_params=pltpu.CompilerParams(
            collective_id=0, has_side_effects=True, vmem_limit_bytes=62 * 1024 * 1024
        ),
        cost_estimate=pl.CostEstimate(flops=flops, bytes_accessed=4 * 1024 * 1024, transcendentals=0),
    )(
        flat(state),
        flat(observed),
        flat(obs_mask),
        flat(noise),
        jnp.transpose(w_first, (2, 3, 1, 0)),
        b_first.reshape(1, hid),
        jnp.transpose(w_second, (2, 3, 0, 1)),
        b_second.reshape(1, nvars),
    )
    return out.reshape(state.shape)


def solution(mesh):
    part = P(("groups", "tm"), None, None, None)
    return jax.shard_map(
        functools.partial(on_device, mesh.shape["tm"]),
        mesh=mesh,
        in_specs=(part, part, part, part, P(), P(), P(), P()),
        out_specs=part,
        check_vma=False,
    )
```

```python
import functools
import math

import jax
import jax.numpy as jnp
from jax import lax
from jax.experimental import pallas as pl
from jax.experimental.pallas import tpu as pltpu
from jax.sharding import PartitionSpec as P

CHUNKS = 2
LANES = 128
ROWS = 16
RADIX = 4


def cut(field, chunks, useful, halo):
    lon = field.shape[-1]
    pieces = []
    for c in range(chunks):
        lo, hi = c * useful - halo, (c + 1) * useful + halo
        parts = []
        if lo < 0:
            parts.append(field[:, lon + lo :])
        parts.append(field[:, max(lo, 0) : min(hi, lon)])
        if hi > lon:
            parts.append(field[:, : hi - lon])
        pieces.append(jnp.concatenate(parts, axis=1) if len(parts) > 1 else parts[0])
    return pieces


def kernel(
    n, chunks, useful, halo,
    state_hbm, obs_hbm, mask_hbm, noise_hbm, w1_hbm, b1_ref, w2_hbm, b2_ref, out_ref,
    state_v, obs_v, mask_v, noise_v, w1_v, w2_v,
    w1t, b1t, b2t, fld, inn, drift, gacc, acc, whole, win, sums,
    local_sem, send_sem, recv_sem, sum_send, sum_recv,
):
    me = lax.axis_index("tm")
    group = lax.axis_index("groups")
    core = lax.rem(me, 2)
    par = lax.rem(me // 2, 2)
    sib = me + 1 - 2 * core
    partner = me + 2 - 4 * par
    onward = me + 4 - 8 * par
    source = me - 4 + 8 * par
    near, far = 4 - 4 * par, 4 * par
    cousin = jnp.where(core == par, sib, onward + 1 - 2 * core)
    has_far = jnp.logical_or(jnp.logical_and(par == 0, me >= 4), jnp.logical_and(par == 1, me + 4 < n))
    has_onward = jnp.logical_or(jnp.logical_and(par == 0, me + 4 < n), jnp.logical_and(par == 1, me >= 4))
    has_cousin = jnp.logical_or(core == par, has_onward)
    nvars = fld.shape[1]
    hid = w1t.shape[0]
    width = fld.shape[2]
    steps = 2 * chunks

    barrier = pltpu.get_barrier_semaphore()

    loads = []
    for i, (src, dst) in enumerate(
        (
            (state_hbm, state_v),
            (w1_hbm.at[w1_hbm.shape[0] // 2], w1_v),
            (w2_hbm.at[w2_hbm.shape[0] // 2], w2_v),
            (obs_hbm, obs_v),
            (mask_hbm, mask_v),
            (noise_hbm, noise_v),
        )
    ):
        loads.append(pltpu.make_async_copy(src, dst, local_sem.at[i]))
        loads[-1].start()

    strides = [RADIX**i for i in range(round(math.log(n, RADIX)))]

    def peer(stride, turn):
        digit = lax.rem(me // stride, RADIX)
        return me + (lax.rem(digit + turn, RADIX) - digit) * stride

    def greet(device):
        pl.semaphore_signal(barrier, inc=1, device_id=(group, device), device_id_type=pl.DeviceIdType.MESH)

    for stride in strides:
        for turn in range(1, RADIX):
            greet(peer(stride, turn))

    @pl.when(has_far)
    def _():
        greet(source)

        @pl.when(core == par)
        def _():
            greet(source + 1 - 2 * core)

    def remote(step, kind, src, dst, device):
        return pltpu.make_async_remote_copy(
            src_ref=win.at[step, src],
            dst_ref=win.at[step, dst],
            send_sem=send_sem.at[step, kind],
            recv_sem=recv_sem.at[step, kind],
            device_id=(group, device),
            device_id_type=pl.DeviceIdType.MESH,
        )

    def direct(step):
        return remote(step, 0, 2, far, partner)

    def forward(step):
        return remote(step, 1, near, far, onward)

    def own_to_sib(step):
        return remote(step, 2, 2, 1 + 2 * core, sib)

    def relay(step):
        return remote(step, 3, near, 3 - 2 * core, cousin)

    @pl.when(jnp.logical_not(has_far))
    def _():
        @pl.loop(0, steps)
        def _(step):
            win[step, far] = jnp.zeros((nvars, width), jnp.bfloat16)

    @pl.when(jnp.logical_and(jnp.logical_not(has_far), core == par))
    def _():
        @pl.loop(0, steps)
        def _(step):
            win[step, 1 + 2 * core] = jnp.zeros((nvars, width), jnp.bfloat16)

    loads[0].wait()

    @pl.loop(0, nvars // ROWS)
    def _(i):
        rows = pl.ds(pl.multiple_of(i * ROWS, ROWS), ROWS)
        for c, piece in enumerate(cut(state_v[rows, 0, :], chunks, useful, halo)):
            fld[c, rows] = piece
            win[c, 2, rows] = piece.astype(jnp.bfloat16)

    extra = jnp.where(has_onward, jnp.where(core == par, 1, 2), 0)
    pl.semaphore_wait(barrier, (RADIX - 1) * len(strides) + extra)

    @pl.loop(0, chunks)
    def _(c):
        direct(c).start()
        own_to_sib(c).start()

    def pass_on(step):
        direct(step).wait_recv()

        @pl.when(has_onward)
        def _():
            forward(step).start()

        @pl.when(has_cousin)
        def _():
            relay(step).start()

    loads[1].wait()

    roles = (2, 3 - 2 * core, near, far, 1 + 2 * core)
    for role, slot in enumerate(roles):
        rows = pl.ds(pl.multiple_of(slot * nvars, nvars), nvars)
        stacked = jnp.concatenate([w1_v[tap, rows, :] for tap in range(3)], axis=0)
        w1t[:, role * 3 * nvars : (role + 1) * 3 * nvars] = stacked.astype(jnp.float32).T.astype(jnp.bfloat16)

    pass_on(0)
    b1t[...] = jnp.broadcast_to(b1_ref[...], (LANES, hid)).T
    b2t[...] = jnp.broadcast_to(b2_ref[...], (LANES, nvars)).T
    loads[2].wait()
    loads[3].wait()
    loads[4].wait()
    loads[5].wait()

    def prepare(i, total):
        rows = pl.ds(pl.multiple_of(i * ROWS, ROWS), ROWS)
        masks = cut(mask_v[rows, 0, :].astype(jnp.float32), chunks, useful, halo)
        seen = cut(obs_v[rows, 0, :], chunks, useful, halo)
        for c in range(chunks):
            inn[0, c, rows] = masks[c]
            inn[1, c, rows] = seen[c]
        noise = noise_v[rows, 0, :]
        whole[2, rows] = noise
        return total + jnp.sum(noise * noise)

    zsq = lax.fori_loop(0, nvars // ROWS, prepare, jnp.float32(0))
    gacc[...] = jnp.zeros_like(gacc)

    def taps(step, slot):
        x = win[step, slot]
        xf = x.astype(jnp.float32)
        return [pltpu.roll(xf, 1, 1).astype(jnp.bfloat16), x, pltpu.roll(xf, width - 1, 1).astype(jnp.bfloat16)]

    lane = lax.broadcasted_iota(jnp.int32, (nvars, width), 1)
    valid = jnp.logical_and(lane >= halo, lane < halo + useful)
    split = 2 * 3 * nvars

    def product(step, first, last, weights):
        stacked = jnp.concatenate([row for role in range(first, last) for row in taps(step, roles[role])], axis=0)
        return jnp.dot(weights, stacked, preferred_element_type=jnp.float32)

    def begin(step, c):
        own_to_sib(step).wait_recv()
        acc[c] = product(step, 0, 2, w1t[:, :split]) + b1t[:, :1]

    def finish(step, c):
        @pl.when(has_far)
        def _():
            forward(step).wait_recv()

        @pl.when(jnp.logical_or(core != par, has_far))
        def _():
            relay(step).wait_recv()

        pre = acc[c] + product(step, 2, 5, w1t[:, split:])
        hidden = (0.5 * pre * (1.0 + jnp.tanh(0.5 * pre))).astype(jnp.bfloat16)
        y = jnp.dot(w2_v[...].reshape(3 * nvars, hid), hidden, preferred_element_type=jnp.float32)
        out = pltpu.roll(y[:nvars], 1, 1) + y[nvars : 2 * nvars] + pltpu.roll(y[2 * nvars :], width - 1, 1)
        field = fld[c]
        return field, out + b2t[:, :1] + inn[0, c] * (inn[1, c] - field)

    @pl.loop(1, chunks)
    def _(c):
        begin(c - 1, c - 1)
        pass_on(c)

    begin(chunks - 1, chunks - 1)

    @pl.loop(0, chunks)
    def _(c):
        field, score = finish(c, c)
        moved = field + 0.5 * score
        fld[c] = moved
        win[c + chunks, 2] = moved.astype(jnp.bfloat16)
        direct(c + chunks).start()
        own_to_sib(c + chunks).start()

        @pl.when(c >= 1)
        def _():
            pass_on(c + chunks - 1)

    @pl.loop(0, chunks - 1)
    def _(c):
        begin(c + chunks, c)

    pass_on(steps - 1)
    begin(steps - 1, chunks - 1)

    @pl.loop(0, chunks)
    def _(c):
        _, score = finish(c + chunks, c)
        drift[c] = score
        gacc[...] += jnp.where(valid, score * score, 0.0)

    gsq = gacc[...]
    def share(stage, turn):
        stride = strides[stage]
        return pltpu.make_async_remote_copy(
            src_ref=sums.at[stage, 0],
            dst_ref=sums.at[stage, turn],
            send_sem=sum_send.at[stage, turn],
            recv_sem=sum_recv.at[stage, turn],
            device_id=(group, peer(stride, turn)),
            device_id_type=pl.DeviceIdType.MESH,
        )

    row = lax.broadcasted_iota(jnp.int32, (8, LANES), 0)
    tot = jnp.where(row == 0, zsq, jnp.sum(gsq))
    for stage in range(len(strides)):
        sums[stage, 0] = tot
        for turn in range(1, RADIX):
            share(stage, turn).start()

        if stage == 0:

            @pl.loop(0, nvars // ROWS)
            def _(i):
                rows = pl.ds(pl.multiple_of(i * ROWS, ROWS), ROWS)
                for c in range(chunks):
                    span = slice(c * useful, (c + 1) * useful)
                    whole[0, rows, span] = fld[c, rows, halo : halo + useful]
                    whole[1, rows, span] = drift[c, rows, halo : halo + useful]

        for turn in range(1, RADIX):
            share(stage, turn).wait_recv()
        tot = (sums[stage, 0] + sums[stage, 2]) + (sums[stage, 1] + sums[stage, 3])

    zall = tot[0:1, 0:1]
    gall = tot[1:2, 0:1]
    size = 2.0 * 0.16 * 0.16 * zall / (gall + 1e-06)
    scale = jnp.sqrt(2.0 * size)

    @pl.loop(0, nvars // ROWS)
    def _(i):
        rows = pl.ds(pl.multiple_of(i * ROWS, ROWS), ROWS)
        out_ref[rows, 0, :] = whole[0, rows] + size * whole[1, rows] + scale * whole[2, rows]

    for stage in range(len(strides)):
        for turn in range(1, RADIX):
            share(stage, turn).wait_send()

    @pl.loop(0, steps)
    def _(step):
        direct(step).wait_send()
        own_to_sib(step).wait_send()

        @pl.when(has_onward)
        def _():
            forward(step).wait_send()

        @pl.when(has_cousin)
        def _():
            relay(step).wait_send()


def on_device(n, state, observed, obs_mask, noise, w_first, b_first, w_second, b_second):
    hours, nvars, lat, lon = state.shape
    hid = w_first.shape[0]
    assert hours == 1 and lat == 1 and n % 4 == 0
    assert w_first.shape[1:] == (5 * nvars, 3, 3)
    chunks = CHUNKS
    padded = -(-(lon + 8 * chunks) // (LANES * chunks)) * LANES * chunks
    width = padded // chunks
    assert lon % chunks == 0
    useful = lon // chunks
    halo = (width - useful) // 2
    assert halo >= 4 and useful + 2 * halo == width and halo <= useful
    flat = lambda a: a.reshape(nvars, 1, lon)
    any_spec = pl.BlockSpec(memory_space=pl.ANY)
    vmem = pl.BlockSpec(memory_space=pltpu.VMEM)
    steps = 2 * chunks
    stages = round(math.log(n, RADIX))
    assert RADIX**stages == n
    flops = 4 * width * chunks * hid * nvars * (15 + 3)
    out = pl.pallas_call(
        functools.partial(kernel, n, chunks, useful, halo),
        out_shape=jax.ShapeDtypeStruct((nvars, 1, lon), jnp.float32),
        in_specs=[any_spec] * 5 + [vmem, any_spec, vmem],
        out_specs=vmem,
        scratch_shapes=[
            pltpu.VMEM((nvars, 1, lon), jnp.float32),
            pltpu.VMEM((nvars, 1, lon), jnp.float32),
            pltpu.VMEM((nvars, 1, lon), jnp.int32),
            pltpu.VMEM((nvars, 1, lon), jnp.float32),
            pltpu.VMEM((3, 5 * nvars, hid), jnp.bfloat16),
            pltpu.VMEM((3, nvars, hid), jnp.bfloat16),
            pltpu.VMEM((hid, 15 * nvars), jnp.bfloat16),
            pltpu.VMEM((hid, LANES), jnp.float32),
            pltpu.VMEM((nvars, LANES), jnp.float32),
            pltpu.VMEM((chunks, nvars, width), jnp.float32),
            pltpu.VMEM((2, chunks, nvars, width), jnp.float32),
            pltpu.VMEM((chunks, nvars, width), jnp.float32),
            pltpu.VMEM((nvars, width), jnp.float32),
            pltpu.VMEM((chunks, hid, width), jnp.float32),
            pltpu.VMEM((3, nvars, lon), jnp.float32),
            pltpu.VMEM((steps, 5, nvars, width), jnp.bfloat16),
            pltpu.VMEM((stages, RADIX, 8, LANES), jnp.float32),
            pltpu.SemaphoreType.DMA((6,)),
            pltpu.SemaphoreType.DMA((steps, 4)),
            pltpu.SemaphoreType.DMA((steps, 4)),
            pltpu.SemaphoreType.DMA((stages, RADIX)),
            pltpu.SemaphoreType.DMA((stages, RADIX)),
        ],
        compiler_params=pltpu.CompilerParams(
            collective_id=0, has_side_effects=True, vmem_limit_bytes=62 * 1024 * 1024
        ),
        cost_estimate=pl.CostEstimate(flops=flops, bytes_accessed=4 * 1024 * 1024, transcendentals=0),
    )(
        flat(state),
        flat(observed),
        flat(obs_mask),
        flat(noise),
        jnp.transpose(w_first, (2, 3, 1, 0)),
        b_first.reshape(1, hid),
        jnp.transpose(w_second, (2, 3, 0, 1)),
        b_second.reshape(1, nvars),
    )
    return out.reshape(state.shape)


def solution(mesh):
    part = P(("groups", "tm"), None, None, None)
    return jax.shard_map(
        functools.partial(on_device, mesh.shape["tm"]),
        mesh=mesh,
        in_specs=(part, part, part, part, P(), P(), P(), P()),
        out_specs=part,
        check_vma=False,
    )
```
